512 devices in a mesh: outer: 16 (over z, y_lo), inner: 32 (over x, y_hi, core).
Axes of the slice: x: 4, y: 8 (y_hi: 4, y_lo: 2; y = y_hi * 2 + y_lo), z: 8, core: 2. Of those that a mesh axis runs over, the one named last changes fastest.
Arguments:
- queries: bfloat16 [131072, 1024], P(('outer', 'inner')), may hold values from -6 to 6
- keys: bfloat16 [131072, 128], P(('outer', 'inner')), may hold values from -6 to 6
- values: bfloat16 [131072, 128], P(('outer', 'inner')), may hold values from -6 to 6
- outputs: bfloat16 [131072, 1024], P(('outer', 'inner')), may hold values from -1.5 to 1.5
- out_grads: bfloat16 [131072, 1024], P(('outer', 'inner')), may hold values from -48 to 48
- log_sum_exp: float32 [8, 131072], P(None, ('outer', 'inner')), may hold values from 5 to 7
- span_ids: int32 [2, 512], replicated, may hold values from 0 to 1023, as said below
Outputs:
- query_grads: float32 [131072, 1024], P(('outer', 'inner'))
- key_grads: float32 [131072, 128], P(('outer', 'inner'))
- value_grads: float32 [131072, 128], P(('outer', 'inner'))
The draws below stay inside these ranges and needn't reach their ends.
Inputs may be any that keep to these rules, and one draw needn't show every extreme that they name: `span_ids`: column b holds two span numbers c and 1023 - c; each number from 0 to 1023 stands once in the array.
All inputs are finite; a program needn't handle non-finite values.
Results may differ from the reference program's by a relative error of at most 0.0042.
Values may be sent and summed in bfloat16 or wider, within the bound.
A program may use at most 64 MiB of HBM per device.

```python
import jax
import jax.numpy as jnp
from jax import lax

HEADS = 8
HEAD_DIM = 128
TOK_DEV = 256
INNER_STEPS = 4
HALF = 128
INNER_BLOCKS = 32
OUTER_BLOCKS = 16
BLOCKS = 512
TOKENS = 131072


def draw_span_ids(key, part):
    key = jax.random.fold_in(key, 11)
    shuffled = jax.random.permutation(key, BLOCKS).astype(jnp.int32)
    return jnp.stack([shuffled, 2 * BLOCKS - 1 - shuffled]).astype(jnp.int32)


def shard_levels(key, shape, cuts, least, high):
    def one(axis_at, shards_of):
        heights = jax.random.uniform(jax.random.fold_in(jax.random.fold_in(key, 6), axis_at), (shards_of,), jnp.float32, least / len(cuts), high / len(cuts))
        return jnp.repeat(jnp.exp(heights), shape[axis_at] // shards_of).reshape((-1,) + (1,) * (len(shape) - axis_at - 1))

    loudness = one(*cuts[0])
    for cut in cuts[1:]:
        loudness = loudness * one(*cut)
    return loudness


def centred(key, dims, spread, most, cuts=(), held_as=jnp.bfloat16):
    loudness = shard_levels(key, dims, cuts, -0.22, 0.18) if cuts else 1.0
    values = jax.random.normal(key, dims, jnp.float32) * spread * loudness
    return jnp.minimum(jnp.maximum(values, -most), most).astype(held_as)


def setup_inputs(seed: int = 0) -> dict:
    arg_keys = jax.random.split(jax.random.key(seed), 8)
    return {
        "queries": centred(arg_keys[0], (TOKENS, HEADS * HEAD_DIM), 1.0, 6.0, ((0, 512),)),
        "keys": centred(arg_keys[1], (TOKENS, HEAD_DIM), 1.0, 6.0, ((0, 512),)),
        "values": centred(arg_keys[2], (TOKENS, HEAD_DIM), 1.0, 6.0, ((0, 512),)),
        "outputs": centred(arg_keys[3], (TOKENS, HEADS * HEAD_DIM), 0.25, 1.5, ((0, 512),)),
        "out_grads": centred(arg_keys[4], (TOKENS, HEADS * HEAD_DIM), 8.0, 48.0, ((0, 512),)),
        "log_sum_exp": jnp.clip(5.0 + 2.0 * jax.random.uniform(arg_keys[5], (HEADS, TOKENS), jnp.float32) ** shard_levels(arg_keys[5], (HEADS, TOKENS), ((1, 512),), -0.2, 0.2), 5.0, 7.0),
        "span_ids": draw_span_ids(jax.random.fold_in(arg_keys[7], 71), 0),
    }


def pair_grads(query_heads, grad_heads, log_norm, deltas, key_block, value_block, query_place, key_place):
    scaling = HEAD_DIM ** -0.5
    exact = lax.Precision.HIGHEST
    query_wide = query_heads.astype(jnp.float32)
    grad_wide = grad_heads.astype(jnp.float32)
    key_wide = key_block.astype(jnp.float32)
    value_wide = value_block.astype(jnp.float32)
    scores = jnp.einsum("qhd,kd->hqk", query_wide, key_wide, precision=exact) * scaling
    allowed = key_place[None, None, :] <= query_place[None, :, None]
    attend = jnp.where(allowed, jnp.exp(scores - log_norm[:, :, None]), jnp.float32(0.0))
    attend_low = lax.optimization_barrier(attend.astype(jnp.bfloat16)).astype(jnp.float32)
    grad_value = jnp.einsum("hqk,qhd->kd", attend_low, grad_wide, precision=exact)
    grad_attend = jnp.einsum("qhd,kd->hqk", grad_wide, value_wide, precision=exact)
    grad_scores = attend * (grad_attend - deltas[:, :, None])
    grad_scores = lax.optimization_barrier(grad_scores.astype(jnp.bfloat16)).astype(jnp.float32)
    grad_query = jnp.einsum("hqk,kd->qhd", grad_scores, key_wide, precision=exact) * scaling
    grad_key = jnp.einsum("hqk,qhd->kd", grad_scores, query_wide, precision=exact) * scaling
    return grad_query, grad_key, grad_value


def to_grid(array):
    return array.reshape((OUTER_BLOCKS, INNER_BLOCKS) + array.shape[1:])


def to_flat(array):
    return array.reshape((BLOCKS,) + array.shape[2:])


def reference(queries, keys, values, outputs, out_grads, log_sum_exp, span_ids):
    query_heads = queries.reshape(BLOCKS, TOK_DEV, HEADS, HEAD_DIM)
    grad_heads = out_grads.reshape(BLOCKS, TOK_DEV, HEADS, HEAD_DIM)
    out_heads = outputs.reshape(BLOCKS, TOK_DEV, HEADS, HEAD_DIM)
    deltas = jnp.sum(grad_heads.astype(jnp.float32) * out_heads.astype(jnp.float32), axis=3).transpose(0, 2, 1)
    log_norm = log_sum_exp.reshape(HEADS, BLOCKS, TOK_DEV).transpose(1, 0, 2)
    key_rows = keys.reshape(BLOCKS, TOK_DEV, HEAD_DIM)
    value_rows = values.reshape(BLOCKS, TOK_DEV, HEAD_DIM)
    starts = (span_ids * HALF).astype(jnp.int32).T
    places = (starts[:, :, None] + jnp.arange(HALF, dtype=jnp.int32)[None, None, :]).reshape(BLOCKS, TOK_DEV)
    moves = [(1, offset) for offset in range(INNER_STEPS + 1)] + [(0, 1)]
    query_acc = jnp.zeros((BLOCKS, TOK_DEV, HEADS, HEAD_DIM), jnp.float32)
    key_acc = jnp.zeros((BLOCKS, TOK_DEV, HEAD_DIM), jnp.float32)
    value_acc = jnp.zeros((BLOCKS, TOK_DEV, HEAD_DIM), jnp.float32)
    for roll_axis, roll_by in moves:
        key_moved = to_flat(jnp.roll(to_grid(key_rows), roll_by, roll_axis))
        value_moved = to_flat(jnp.roll(to_grid(value_rows), roll_by, roll_axis))
        place_moved = to_flat(jnp.roll(to_grid(places), roll_by, roll_axis))
        grad_query, grad_key, grad_value = lax.map(
            lambda operands: pair_grads(*operands),
            (query_heads, grad_heads, log_norm, deltas, key_moved, value_moved, places, place_moved))
        query_acc = query_acc + grad_query
        key_acc = key_acc + to_flat(jnp.roll(to_grid(grad_key), -roll_by, roll_axis))
        value_acc = value_acc + to_flat(jnp.roll(to_grid(grad_value), -roll_by, roll_axis))
    return (query_acc.reshape(TOKENS, HEADS * HEAD_DIM),
            key_acc.reshape(TOKENS, HEAD_DIM),
            value_acc.reshape(TOKENS, HEAD_DIM))
```

```python
import functools
import math

import jax
import jax.numpy as jnp
from jax import lax
from jax.experimental import pallas as pl
from jax.experimental.pallas import tpu as pltpu
from jax.sharding import PartitionSpec as P

MESH = pl.DeviceIdType.MESH
HALF = 128
DIM = 128
HEADS = 8
PAIR = 256
NT = (((1,), (1,)), ((), ()))
NN = (((1,), (0,)), ((), ()))
TN = (((0,), (0,)), ((), ()))
LOG2E = math.log2(math.e)

OWN, TWO, FOUR, ONE, THREE, OUTER = range(6)


def dot(a, b, dims):
    return lax.dot_general(a, b, dims, preferred_element_type=jnp.float32)


def kernel(
    n_outer,
    n_inner,
    spans,
    q_hbm,
    k_hbm,
    v_hbm,
    o_hbm,
    g_hbm,
    lse_hbm,
    dq_hbm,
    dk_hbm,
    dv_hbm,
    q_in,
    k_in,
    v_in,
    o_in,
    g_in,
    lse_in,
    qn,
    gn,
    rows,
    kv,
    dq,
    acc,
    own_acc,
    gout,
    gin,
    dq_out,
    dkv_out,
    load_sem,
    store_sem,
    kv_send,
    kv_recv,
    g_send,
    g_recv,
):
    outer = lax.axis_index("outer")
    inner = lax.axis_index("inner")
    core = lax.rem(inner, 2)
    scale = DIM ** (-0.5)

    def at(do, di):
        return (lax.rem(outer + do + n_outer, n_outer), lax.rem(inner + di + n_inner, n_inner))

    partner = (outer, inner + 1 - 2 * core)
    friends = [at(0, 2), at(0, -2), at(0, 4), at(0, -4), at(1, 0), at(-1, 0), partner]

    loads = [
        pltpu.make_async_copy(src, dst, load_sem.at[n])
        for n, (src, dst) in enumerate(
            [
                (k_hbm, k_in),
                (v_hbm, v_in),
                (g_hbm, g_in),
                (o_hbm, o_in),
                (q_hbm, q_in),
                (lse_hbm, lse_in),
            ]
        )
    ]
    for copy in loads:
        copy.start()

    barrier = pltpu.get_barrier_semaphore()
    for friend in friends:
        pl.semaphore_signal(barrier, inc=1, device_id=friend, device_id_type=MESH)

    def low_span(block):
        return jnp.minimum(spans[0, block], spans[1, block])

    def less(a, b, shape):
        return jnp.full(shape, a, jnp.int32) < jnp.full(shape, b, jnp.int32)

    def narrow(mask):
        return jnp.where(mask, 1.0, 0.0).astype(jnp.bfloat16) > 0.5

    def either(mask, yes, no):
        return jnp.where(mask, yes, no)

    own_block = outer * n_inner + inner
    own_low = low_span(own_block)
    swapped = less(spans[1, own_block], spans[0, own_block], (HALF, DIM))
    swapped_low = narrow(swapped)

    def by_span(first, second, half, mask):
        return either(mask, *((second, first) if half == 0 else (first, second)))

    def kv_copy(part, slot_from, slot_to, number, target):
        return pltpu.make_async_remote_copy(
            src_ref=kv.at[slot_from, part],
            dst_ref=kv.at[slot_to, part],
            send_sem=kv_send.at[number, part],
            recv_sem=kv_recv.at[slot_to, part],
            device_id=target,
            device_id_type=MESH,
        )

    to_four = [kv_copy(p, OWN, FOUR, 0, at(0, 4)) for p in range(2)]
    to_two = [kv_copy(p, OWN, TWO, 1, at(0, 2)) for p in range(2)]
    to_outer = [kv_copy(p, OWN, OUTER, 2, at(1, 0)) for p in range(2)]
    to_one = [kv_copy(p, core, ONE, 3, partner) for p in range(2)]
    to_three = [kv_copy(p, core + 1, THREE, 4, partner) for p in range(2)]

    for part, (copy, ref) in enumerate([(loads[0], k_in), (loads[1], v_in)]):
        copy.wait()
        for half in range(2):
            kv[OWN, part, pl.ds(half * HALF, HALF), :] = by_span(
                ref[:HALF, :], ref[HALF:, :], half, swapped_low
            )
    pl.semaphore_wait(barrier, len(friends))
    for part in range(2):
        to_four[part].start()
        to_two[part].start()
        to_outer[part].start()

        @pl.when(core == 0)
        def _():
            to_one[part].start()

    for copy in loads[2:]:
        copy.wait()
    ones = jnp.ones((8, DIM), jnp.bfloat16)
    for half in range(2):

        def prepare(h, carry, half=half):
            col = pl.ds(pl.multiple_of(h * DIM, DIM), DIM)

            def halved(ref):
                return by_span(ref[pl.ds(0, HALF), col], ref[pl.ds(HALF, HALF), col], half, swapped_low)

            grad = halved(g_in)
            qn[half, col, :] = halved(q_in)
            gn[half, col, :] = grad
            product = grad.astype(jnp.float32) * halved(o_in).astype(jnp.float32)
            top = product.astype(jnp.bfloat16)
            rest = product - top.astype(jnp.float32)
            middle = rest.astype(jnp.bfloat16)
            low = (rest - middle.astype(jnp.float32)).astype(jnp.bfloat16)
            delta = dot(ones, top, NT) + dot(ones, middle, NT) + dot(ones, low, NT)
            rows[half, 0:1, col] = delta[0:1, :]
            return carry

        lax.fori_loop(0, HEADS, prepare, 0)
        for h in range(HEADS):
            rows[half, 1:2, pl.ds(h * DIM, DIM)] = LOG2E * by_span(
                lse_in[h : h + 1, :HALF], lse_in[h : h + 1, HALF:], half, swapped[:1]
            )

    def attend(keys, q, norm):
        return jnp.exp2(dot(keys, q, NT) * (scale * LOG2E) - norm)

    def score_grads(p, values, g, delta):
        return (p * (dot(values, g, NT) - delta)).astype(jnp.bfloat16)

    key_at = lax.broadcasted_iota(jnp.int32, (HALF, PAIR), 0)
    query_at = lax.rem(lax.broadcasted_iota(jnp.int32, (HALF, PAIR), 1), HALF)
    seen = key_at <= query_at
    own_acc[...] = jnp.zeros_like(own_acc)

    def own_step(step, carry):
        cols = pl.ds(pl.multiple_of(step * PAIR, PAIR), PAIR)
        keys = kv[OWN, 0]
        values = kv[OWN, 1]
        q_lo, q_hi = qn[0, cols, :], qn[1, cols, :]
        g_lo, g_hi = gn[0, cols, :], gn[1, cols, :]
        p_lo = jnp.where(seen, attend(keys[:HALF], q_lo, rows[0, 1:2, cols]), 0.0)
        p_hi = attend(keys, q_hi, rows[1, 1:2, cols])
        p_hi = jnp.concatenate([p_hi[:HALF], jnp.where(seen, p_hi[HALF:], 0.0)], 0)
        own_acc[1] += dot(p_hi.astype(jnp.bfloat16), g_hi, NN)
        own_acc[1, pl.ds(0, HALF), :] += dot(p_lo.astype(jnp.bfloat16), g_lo, NN)
        s_lo = score_grads(p_lo, values[:HALF], g_lo, rows[0, 0:1, cols])
        s_hi = score_grads(p_hi, values, g_hi, rows[1, 0:1, cols])
        own_acc[0] += dot(s_hi, q_hi, NN)
        own_acc[0, pl.ds(0, HALF), :] += dot(s_lo, q_lo, NN)
        dq[cols, pl.ds(0, DIM)] = dot(s_lo, keys[:HALF], TN)
        dq[cols, pl.ds(DIM, DIM)] = dot(s_hi, keys, TN)
        return carry

    lax.fori_loop(0, HEADS * HALF // PAIR, own_step, 0)

    def other(slot, block):
        early = less(low_span(block), own_low, (HALF, DIM))
        early_low = narrow(less(low_span(block), own_low, (PAIR, DIM)))
        early_row = less(low_span(block), own_low, (1, PAIR))
        acc[...] = jnp.zeros_like(acc)

        def step_of(step, carry):
            cols = pl.ds(pl.multiple_of(step * PAIR, PAIR), PAIR)
            k1, v1 = kv[slot, 0, pl.ds(0, HALF), :], kv[slot, 1, pl.ds(0, HALF), :]
            k2 = either(early_low[:HALF], k1, kv[slot, 0, pl.ds(HALF, HALF), :])
            v2 = either(early_low[:HALF], v1, kv[slot, 1, pl.ds(HALF, HALF), :])
            q1, g1 = qn[1, cols, :], gn[1, cols, :]
            q2 = either(early_low, qn[0, cols, :], q1)
            g2 = either(early_low, gn[0, cols, :], g1)
            norm1, delta1 = rows[1, 1:2, cols], rows[1, 0:1, cols]
            norm2 = either(early_row, rows[0, 1:2, cols], norm1)
            delta2 = either(early_row, rows[0, 0:1, cols], delta1)
            p1 = attend(k1, q1, norm1)
            p2 = attend(k2, q2, norm2)
            acc[0, 1] += dot(p1.astype(jnp.bfloat16), g1, NN)
            acc[1, 1] += dot(p2.astype(jnp.bfloat16), g2, NN)
            s1 = score_grads(p1, v1, g1, delta1)
            s2 = score_grads(p2, v2, g2, delta2)
            acc[0, 0] += dot(s1, q1, NN)
            acc[1, 0] += dot(s2, q2, NN)
            zero = jnp.zeros_like(k1)
            wide = jnp.concatenate(
                [
                    jnp.concatenate([zero, k1], 1),
                    jnp.concatenate(
                        [either(early_low[:HALF], k2, zero), either(early_low[:HALF], zero, k2)], 1
                    ),
                ],
                0,
            )
            dq[cols, :] += dot(jnp.concatenate([s1, s2], 0), wide, TN)
            return carry

        lax.fori_loop(0, HEADS * HALF // PAIR, step_of, 0)
        result = []
        for part in range(2):
            first, second = acc[0, part], acc[1, part]
            result.append(
                (
                    first + jnp.where(early, second, 0.0),
                    jnp.where(early, 0.0, second),
                )
            )
        return result

    def block_at(do, di):
        there = at(do, di)
        return there[0] * n_inner + there[1]

    def put(slot, grads, extra=None):
        for part in range(2):
            for half in range(2):
                where = pl.ds(half * HALF, HALF)
                value = grads[part][half]
                if extra is not None:
                    value = value + gin[extra, part, where, :].astype(jnp.float32)
                gout[slot, part, where, :] = value.astype(jnp.bfloat16)

    def g_copy(slot, target):
        return pltpu.make_async_remote_copy(
            src_ref=gout.at[slot],
            dst_ref=gin.at[slot],
            send_sem=g_send.at[slot],
            recv_sem=g_recv.at[slot],
            device_id=target,
            device_id_type=MESH,
        )

    g_two = g_copy(TWO, at(0, -2))
    g_four = g_copy(FOUR, at(0, -4))
    g_outer = g_copy(OUTER, at(-1, 0))
    g_one = g_copy(ONE, partner)
    g_three = g_copy(THREE, partner)

    def add_to(slot, extra):
        gout[slot] = (gout[slot].astype(jnp.float32) + gin[extra].astype(jnp.float32)).astype(
            jnp.bfloat16
        )

    def both_recv(copies):
        for copy in copies:
            copy.wait_recv()

    both_recv(to_two)

    @pl.when(core == 0)
    def _():
        for copy in to_three:
            copy.start()

    @pl.when(core == 1)
    def _():
        for copy in to_one:
            copy.start()

    both_recv(to_outer)
    put(OUTER, other(OUTER, block_at(-1, 0)))
    g_outer.start()
    both_recv(to_four)

    @pl.when(core == 1)
    def _():
        for copy in to_three:
            copy.start()

    put(TWO, other(TWO, block_at(0, -2)))
    both_recv(to_one)
    put(ONE, other(ONE, block_at(0, -1)))
    g_one.start()
    both_recv(to_three)
    put(THREE, other(THREE, block_at(0, -3)))
    g_three.start()
    put(FOUR, other(FOUR, block_at(0, -4)))
    g_one.wait_recv()
    g_three.wait_recv()

    @pl.when(core == 0)
    def _():
        add_to(TWO, THREE)

    @pl.when(core == 1)
    def _():
        add_to(TWO, ONE)
        add_to(FOUR, THREE)

    g_four.start()
    g_two.start()

    for half in range(2):

        def finish(h, carry, half=half):
            head = pl.ds(pl.multiple_of(h * DIM, DIM), DIM)
            value = by_span(dq[head, pl.ds(0, DIM)], dq[head, pl.ds(DIM, DIM)], half, swapped)
            dq_out[pl.ds(half * HALF, HALF), head] = value * scale
            return carry

        lax.fori_loop(0, HEADS, finish, 0)
    store_dq = pltpu.make_async_copy(dq_out, dq_hbm, store_sem.at[0])
    store_dq.start()

    @pl.when(core == 0)
    def _():
        for part in range(2):
            own_acc[part] += gin[ONE, part].astype(jnp.float32)

    g_outer.wait_recv()
    g_two.wait_recv()
    g_four.wait_recv()
    for part in range(2):
        total = own_acc[part]
        for slot in (OUTER, TWO, FOUR):
            total = total + gin[slot, part].astype(jnp.float32)
        if part == 0:
            total = total * scale
        lo, hi = total[:HALF], total[HALF:]
        dkv_out[part, pl.ds(0, HALF), :] = by_span(lo, hi, 0, swapped)
        dkv_out[part, pl.ds(HALF, HALF), :] = by_span(lo, hi, 1, swapped)
    stores = [
        pltpu.make_async_copy(dkv_out.at[0], dk_hbm, store_sem.at[1]),
        pltpu.make_async_copy(dkv_out.at[1], dv_hbm, store_sem.at[2]),
    ]
    for copy in stores:
        copy.start()
    for copies in (to_four, to_two, to_outer, to_one, to_three):
        for copy in copies:
            copy.wait_send()
    for copy in (g_two, g_four, g_outer, g_one, g_three):
        copy.wait_send()
    store_dq.wait()
    for copy in stores:
        copy.wait()


def local(n_outer, n_inner, queries, keys, values, outputs, out_grads, log_sum_exp, span_ids):
    block, dim = keys.shape
    width = queries.shape[1]
    heads = log_sum_exp.shape[0]
    bf16, f32 = jnp.bfloat16, jnp.float32
    in_hbm = pl.BlockSpec(memory_space=pl.ANY)
    return pl.pallas_call(
        functools.partial(kernel, n_outer, n_inner),
        out_shape=(
            jax.ShapeDtypeStruct((block, width), f32),
            jax.ShapeDtypeStruct((block, dim), f32),
            jax.ShapeDtypeStruct((block, dim), f32),
        ),
        in_specs=[pl.BlockSpec(memory_space=pltpu.SMEM)] + [in_hbm] * 6,
        out_specs=(in_hbm,) * 3,
        scratch_shapes=[
            pltpu.VMEM((block, width), bf16),
            pltpu.VMEM((block, dim), bf16),
            pltpu.VMEM((block, dim), bf16),
            pltpu.VMEM((block, width), bf16),
            pltpu.VMEM((block, width), bf16),
            pltpu.VMEM((heads, block), f32),
            pltpu.VMEM((2, heads * HALF, dim), bf16),
            pltpu.VMEM((2, heads * HALF, dim), bf16),
            pltpu.VMEM((2, 8, heads * HALF), f32),
            pltpu.VMEM((6, 2, block, dim), bf16),
            pltpu.VMEM((heads * HALF, 2 * dim), f32),
            pltpu.VMEM((2, 2, HALF, dim), f32),
            pltpu.VMEM((2, block, dim), f32),
            pltpu.VMEM((6, 2, block, dim), bf16),
            pltpu.VMEM((6, 2, block, dim), bf16),
            pltpu.VMEM((block, width), f32),
            pltpu.VMEM((2, block, dim), f32),
            pltpu.SemaphoreType.DMA((6,)),
            pltpu.SemaphoreType.DMA((3,)),
            pltpu.SemaphoreType.DMA((5, 2)),
            pltpu.SemaphoreType.DMA((6, 2)),
            pltpu.SemaphoreType.DMA((6,)),
            pltpu.SemaphoreType.DMA((6,)),
        ],
        compiler_params=pltpu.CompilerParams(
            collective_id=0, has_side_effects=True, vmem_limit_bytes=40 * 1024 * 1024
        ),
        name="backward",
    )(span_ids, queries, keys, values, outputs, out_grads, log_sum_exp)


def solution(mesh):
    tokens = P(("outer", "inner"), None)
    return jax.shard_map(
        functools.partial(local, mesh.shape["outer"], mesh.shape["inner"]),
        mesh=mesh,
        in_specs=(tokens,) * 5 + (P(None, ("outer", "inner")), P()),
        out_specs=(tokens,) * 3,
        check_vma=False,
    )
```

```python
import functools
import math

import jax
import jax.numpy as jnp
from jax import lax
from jax.experimental import pallas as pl
from jax.experimental.pallas import tpu as pltpu
from jax.sharding import PartitionSpec as P

MESH = pl.DeviceIdType.MESH
HALF = 128
DIM = 128
HEADS = 8
WIDE = HEADS * HALF
NT = (((1,), (1,)), ((), ()))
NN = (((1,), (0,)), ((), ()))
TN = (((0,), (0,)), ((), ()))
LOG2E = math.log2(math.e)
SCALE = DIM ** (-0.5)

OWN, ONE, TWO, THREE, FOUR, OUTER = range(6)


def dot(a, b, dims):
    return lax.dot_general(a, b, dims, preferred_element_type=jnp.float32)


def less(a, b, shape):
    return jnp.full(shape, a, jnp.int32) < jnp.full(shape, b, jnp.int32)


def narrow(mask):
    return jnp.where(mask, 1.0, 0.0).astype(jnp.bfloat16) > 0.5


def ordered(swapped, first, second):
    return jnp.where(swapped, second, first), jnp.where(swapped, first, second)


def kernel(
    n_outer,
    n_inner,
    spans,
    q_hbm,
    k_hbm,
    v_hbm,
    o_hbm,
    g_hbm,
    lse_hbm,
    dq_out,
    dk_out,
    dv_out,
    q_in,
    o_in,
    g_in,
    lse_in,
    qn,
    gn,
    rows,
    kv,
    dq,
    own_acc,
    gout,
    gin,
    load_sem,
    kv_send,
    kv_recv,
    g_send,
    g_recv,
):
    outer = lax.axis_index("outer")
    inner = lax.axis_index("inner")
    core = lax.rem(inner, 2)

    def at(do, di):
        return (lax.rem(outer + do + n_outer, n_outer), lax.rem(inner + di + n_inner, n_inner))

    partner = (outer, inner + 1 - 2 * core)
    friends = [at(0, 2), at(0, -2), at(0, 4), at(0, -4), at(1, 0), at(-1, 0), partner]

    barrier = pltpu.get_barrier_semaphore()
    for friend in friends:
        pl.semaphore_signal(barrier, inc=1, device_id=friend, device_id_type=MESH)

    loads = [
        pltpu.make_async_copy(src, dst, load_sem.at[n])
        for n, (src, dst) in enumerate(
            [
                (g_hbm, g_in),
                (o_hbm, o_in),
                (q_hbm, q_in),
                (lse_hbm, lse_in),
                (k_hbm, kv.at[OWN, 0]),
                (v_hbm, kv.at[OWN, 1]),
            ]
        )
    ]
    for copy in loads:
        copy.start()

    def low_span(block):
        return jnp.minimum(spans[0, block], spans[1, block])

    def is_swapped(block, shape):
        return less(spans[1, block], spans[0, block], shape)

    own_block = outer * n_inner + inner
    own_low = low_span(own_block)
    swapped = is_swapped(own_block, (HALF, DIM))
    swapped_low = narrow(swapped)

    def kv_copies(sources, slot, number, target):
        return [
            pltpu.make_async_remote_copy(
                src_ref=sources[part],
                dst_ref=kv.at[slot, part],
                send_sem=kv_send.at[number, part],
                recv_sem=kv_recv.at[slot, part],
                device_id=target,
                device_id_type=MESH,
            )
            for part in range(2)
        ]

    args = [k_hbm, v_hbm]
    to_four = kv_copies(args, FOUR, 0, at(0, 4))
    to_two = kv_copies(args, TWO, 1, at(0, 2))
    to_outer = kv_copies(args, OUTER, 2, at(1, 0))
    even_one = kv_copies(args, ONE, 3, partner)
    even_three = kv_copies([kv.at[TWO, p] for p in range(2)], THREE, 4, partner)
    odd_one = kv_copies([kv.at[TWO, p] for p in range(2)], ONE, 3, partner)
    odd_three = kv_copies([kv.at[FOUR, p] for p in range(2)], THREE, 4, partner)

    def start(copies):
        for copy in copies:
            copy.start()

    def received(slot):
        for part in range(2):
            pltpu.make_async_remote_copy(
                src_ref=kv.at[slot, part],
                dst_ref=kv.at[slot, part],
                send_sem=kv_send.at[0, part],
                recv_sem=kv_recv.at[slot, part],
                device_id=partner,
                device_id_type=MESH,
            ).wait_recv()

    pl.semaphore_wait(barrier, len(friends))
    start(to_four)

    @pl.when(core == 0)
    def _():
        start(even_one)

    start(to_two)
    start(to_outer)

    for copy in loads:
        copy.wait()
    ones = jnp.ones((8, DIM), jnp.bfloat16)
    for h in range(HEADS):
        col = pl.ds(h * DIM, DIM)
        row = pl.ds(h * HALF, HALF)

        def halves(ref):
            return ordered(swapped_low, ref[pl.ds(0, HALF), col], ref[pl.ds(HALF, HALF), col])

        norms = ordered(swapped[:1], lse_in[h : h + 1, :HALF], lse_in[h : h + 1, HALF:])
        for half, (q, g, o, norm) in enumerate(zip(halves(q_in), halves(g_in), halves(o_in), norms)):
            qn[half, row, :] = q
            gn[half, row, :] = g
            product = g.astype(jnp.float32) * o.astype(jnp.float32)
            top = product.astype(jnp.bfloat16)
            rest = product - top.astype(jnp.float32)
            middle = rest.astype(jnp.bfloat16)
            low = (rest - middle.astype(jnp.float32)).astype(jnp.bfloat16)
            delta = dot(ones, top, NT) + dot(ones, middle, NT) + dot(ones, low, NT)
            rows[half, 0:1, row] = delta[0:1, :]
            rows[half, 1:2, row] = norm * LOG2E

    def attend(keys, q, norm):
        return jnp.exp2(dot(keys, q, NT) * (SCALE * LOG2E) - norm)

    def score_grads(p, values, g, delta):
        return (p * (dot(values, g, NT) - delta)).astype(jnp.bfloat16)

    def halves_of(slot, part, mask):
        return ordered(mask, kv[slot, part, pl.ds(0, HALF), :], kv[slot, part, pl.ds(HALF, HALF), :])

    def own():
        key_at = lax.broadcasted_iota(jnp.int32, (HALF, WIDE), 0)
        query_at = lax.rem(lax.broadcasted_iota(jnp.int32, (HALF, WIDE), 1), HALF)
        seen = key_at <= query_at
        k_lo, k_hi = halves_of(OWN, 0, swapped_low)
        v_lo, v_hi = halves_of(OWN, 1, swapped_low)
        keys = jnp.concatenate([k_lo, k_hi], 0)
        values = jnp.concatenate([v_lo, v_hi], 0)
        p_lo = jnp.where(seen, attend(k_lo, qn[0], rows[0, 1:2, :]), 0.0)
        p_hi = attend(keys, qn[1], rows[1, 1:2, :])
        p_hi = jnp.concatenate([p_hi[:HALF], jnp.where(seen, p_hi[HALF:], 0.0)], 0)
        s_lo = score_grads(p_lo, v_lo, gn[0], rows[0, 0:1, :])
        s_hi = score_grads(p_hi, values, gn[1], rows[1, 0:1, :])
        for part, (lo, hi, other_side) in enumerate(
            [(s_lo, s_hi, qn), (p_lo.astype(jnp.bfloat16), p_hi.astype(jnp.bfloat16), gn)]
        ):
            total = dot(hi, other_side[1], NN)
            first = total[:HALF] + dot(lo, other_side[0], NN)
            own_acc[part, pl.ds(0, HALF), :], own_acc[part, pl.ds(HALF, HALF), :] = ordered(
                swapped, first, total[HALF:]
            )
        dq[:, pl.ds(0, DIM)] = dot(s_lo, k_lo, TN)
        dq[:, pl.ds(DIM, DIM)] = dot(s_hi, keys, TN)

    def other(slot, do, di):
        there = at(do, di)
        block = there[0] * n_inner + there[1]
        low = low_span(block)
        early = less(low, own_low, (HALF, DIM))
        early_low = narrow(less(low, own_low, (WIDE, DIM)))
        early_row = less(low, own_low, (1, WIDE))
        turned = is_swapped(block, (HALF, DIM))
        turned_low = narrow(turned)
        k1, k_hi = halves_of(slot, 0, turned_low)
        v1, v_hi = halves_of(slot, 1, turned_low)
        k2 = jnp.where(early_low[:HALF], k1, k_hi)
        v2 = jnp.where(early_low[:HALF], v1, v_hi)
        q1, g1 = qn[1], gn[1]
        q2 = jnp.where(early_low, qn[0], q1)
        g2 = jnp.where(early_low, gn[0], g1)
        norm1, delta1 = rows[1, 1:2, :], rows[1, 0:1, :]
        norm2 = jnp.where(early_row, rows[0, 1:2, :], norm1)
        delta2 = jnp.where(early_row, rows[0, 0:1, :], delta1)
        p1 = attend(k1, q1, norm1)
        p2 = attend(k2, q2, norm2)
        s1 = score_grads(p1, v1, g1, delta1)
        s2 = score_grads(p2, v2, g2, delta2)
        for part, (first, second) in enumerate(
            [
                (dot(s1, q1, NN), dot(s2, q2, NN)),
                (dot(p1.astype(jnp.bfloat16), g1, NN), dot(p2.astype(jnp.bfloat16), g2, NN)),
            ]
        ):
            lo = first + jnp.where(early, second, 0.0)
            hi = jnp.where(early, 0.0, second)
            for half, value in enumerate(ordered(turned, lo, hi)):
                gout[slot, part, pl.ds(half * HALF, HALF), :] = value.astype(jnp.bfloat16)
        zero = jnp.zeros_like(k1)
        wide = jnp.concatenate(
            [
                jnp.concatenate([zero, k1], 1),
                jnp.concatenate(
                    [
                        jnp.where(early_low[:HALF], k2, zero),
                        jnp.where(early_low[:HALF], zero, k2),
                    ],
                    1,
                ),
            ],
            0,
        )
        dq[...] += dot(jnp.concatenate([s1, s2], 0), wide, TN)

    def g_copy(slot, target):
        return pltpu.make_async_remote_copy(
            src_ref=gout.at[slot],
            dst_ref=gin.at[slot],
            send_sem=g_send.at[slot],
            recv_sem=g_recv.at[slot],
            device_id=target,
            device_id_type=MESH,
        )

    g_two = g_copy(TWO, at(0, -2))
    g_four = g_copy(FOUR, at(0, -4))
    g_outer = g_copy(OUTER, at(-1, 0))
    g_one = g_copy(ONE, partner)
    g_three = g_copy(THREE, partner)

    def add_to(slot, extra):
        gout[slot] = (gout[slot].astype(jnp.float32) + gin[extra].astype(jnp.float32)).astype(
            jnp.bfloat16
        )

    def pick(even, odd):
        return even + core * (odd - even)

    own()

    slot = pick(FOUR, ONE)
    received(slot)
    other(slot, 0, -slot)

    @pl.when(core == 0)
    def _():
        g_four.start()

    @pl.when(core == 1)
    def _():
        g_one.start()
        received(FOUR)
        start(odd_three)

    @pl.when(core == 0)
    def _():
        received(THREE)

    slot = pick(THREE, FOUR)
    other(slot, 0, -slot)

    @pl.when(core == 0)
    def _():
        g_three.start()

    received(TWO)

    @pl.when(core == 0)
    def _():
        start(even_three)

    @pl.when(core == 1)
    def _():
        start(odd_one)

    other(TWO, 0, -2)

    @pl.when(core == 1)
    def _():
        g_three.wait_recv()
        add_to(FOUR, THREE)
        g_four.start()

    slot = pick(ONE, THREE)
    received(slot)
    other(slot, 0, -slot)

    @pl.when(core == 0)
    def _():
        g_one.start()

    @pl.when(core == 1)
    def _():
        g_three.start()

    received(OUTER)
    other(OUTER, -1, 0)
    g_outer.start()
    g_one.wait_recv()

    @pl.when(core == 0)
    def _():
        g_three.wait_recv()
        add_to(TWO, THREE)

    @pl.when(core == 1)
    def _():
        add_to(TWO, ONE)

    g_two.start()

    for h in range(HEADS):
        row = pl.ds(h * HALF, HALF)
        col = pl.ds(h * DIM, DIM)
        first, second = ordered(swapped, dq[row, pl.ds(0, DIM)], dq[row, pl.ds(DIM, DIM)])
        dq_out[pl.ds(0, HALF), col] = first * SCALE
        dq_out[pl.ds(HALF, HALF), col] = second * SCALE

    @pl.when(core == 0)
    def _():
        for part in range(2):
            own_acc[part] += gin[ONE, part].astype(jnp.float32)

    g_four.wait_recv()
    g_outer.wait_recv()
    g_two.wait_recv()
    for part, (out, factor) in enumerate([(dk_out, SCALE), (dv_out, 1.0)]):
        total = own_acc[part]
        for slot in (FOUR, OUTER, TWO):
            total = total + gin[slot, part].astype(jnp.float32)
        out[...] = total * factor
    for copies in (to_four, to_two, to_outer, odd_one, odd_three):
        for copy in copies:
            copy.wait_send()
    for copy in (g_two, g_four, g_outer, g_one, g_three):
        copy.wait_send()


def write_out(*refs):
    sources, results, sem = refs[:3], refs[3:6], refs[6]
    copies = [
        pltpu.make_async_copy(src, dst, sem.at[n])
        for n, (src, dst) in enumerate(zip(sources, results))
    ]
    for copy in copies:
        copy.start()
    for copy in copies:
        copy.wait()


def local(n_outer, n_inner, queries, keys, values, outputs, out_grads, log_sum_exp, span_ids):
    block, dim = keys.shape
    width = queries.shape[1]
    heads = log_sum_exp.shape[0]
    bf16, f32 = jnp.bfloat16, jnp.float32
    in_hbm = pl.BlockSpec(memory_space=pltpu.HBM)
    in_vmem = pl.BlockSpec(memory_space=pltpu.VMEM)
    arrays = [
        pltpu.with_memory_space_constraint(a, pltpu.HBM)
        for a in (queries, keys, values, outputs, out_grads, log_sum_exp)
    ]
    shapes = [(block, width), (block, dim), (block, dim)]
    grads = pl.pallas_call(
        functools.partial(kernel, n_outer, n_inner),
        out_shape=tuple(pltpu.VMEM(shape, f32) for shape in shapes),
        in_specs=[pl.BlockSpec(memory_space=pltpu.SMEM)] + [in_hbm] * 6,
        out_specs=(in_vmem,) * 3,
        scratch_shapes=[
            pltpu.VMEM((block, width), bf16),
            pltpu.VMEM((block, width), bf16),
            pltpu.VMEM((block, width), bf16),
            pltpu.VMEM((heads, block), f32),
            pltpu.VMEM((2, heads * HALF, dim), bf16),
            pltpu.VMEM((2, heads * HALF, dim), bf16),
            pltpu.VMEM((2, 8, heads * HALF), f32),
            pltpu.VMEM((6, 2, block, dim), bf16),
            pltpu.VMEM((heads * HALF, 2 * dim), f32),
            pltpu.VMEM((2, block, dim), f32),
            pltpu.VMEM((6, 2, block, dim), bf16),
            pltpu.VMEM((6, 2, block, dim), bf16),
            pltpu.SemaphoreType.DMA((6,)),
            pltpu.SemaphoreType.DMA((5, 2)),
            pltpu.SemaphoreType.DMA((6, 2)),
            pltpu.SemaphoreType.DMA((6,)),
            pltpu.SemaphoreType.DMA((6,)),
        ],
        compiler_params=pltpu.CompilerParams(
            collective_id=0, has_side_effects=True, vmem_limit_bytes=48 * 1024 * 1024
        ),
        name="backward",
    )(pltpu.with_memory_space_constraint(span_ids, pltpu.HBM), *arrays)
    return pl.pallas_call(
        write_out,
        out_shape=tuple(jax.ShapeDtypeStruct(shape, f32) for shape in shapes),
        in_specs=[in_vmem] * 3,
        out_specs=(pl.BlockSpec(memory_space=pl.ANY),) * 3,
        scratch_shapes=[pltpu.SemaphoreType.DMA((3,))],
        name="write_out",
    )(*(pltpu.with_memory_space_constraint(a, pltpu.VMEM) for a in grads))


def solution(mesh):
    tokens = P(("outer", "inner"), None)
    return jax.shard_map(
        functools.partial(local, mesh.shape["outer"], mesh.shape["inner"]),
        mesh=mesh,
        in_specs=(tokens,) * 5 + (P(None, ("outer", "inner")), P()),
        out_specs=(tokens,) * 3,
        check_vma=False,
    )
```

```python
import functools
import math

import jax
import jax.numpy as jnp
from jax import lax
from jax.experimental import pallas as pl
from jax.experimental.pallas import tpu as pltpu
from jax.sharding import PartitionSpec as P

MESH = pl.DeviceIdType.MESH
HALF = 128
DIM = 128
HEADS = 8
WIDE = HEADS * HALF
NT = (((1,), (1,)), ((), ()))
NN = (((1,), (0,)), ((), ()))
TN = (((0,), (0,)), ((), ()))
LOG2E = math.log2(math.e)
SCALE = DIM ** (-0.5)

OWN, ONE, TWO, THREE, FOUR, OUTER = range(6)


def dot(a, b, dims):
    return lax.dot_general(a, b, dims, preferred_element_type=jnp.float32)


def less(a, b, shape):
    return jnp.full(shape, a, jnp.int32) < jnp.full(shape, b, jnp.int32)


def narrow(mask):
    return jnp.where(mask, 1.0, 0.0).astype(jnp.bfloat16) > 0.5


def ordered(swapped, first, second):
    return jnp.where(swapped, second, first), jnp.where(swapped, first, second)


def kernel(
    n_outer,
    n_inner,
    spans,
    q_hbm,
    k_hbm,
    v_hbm,
    o_hbm,
    g_hbm,
    lse_hbm,
    dq_out,
    dk_out,
    dv_out,
    q_in,
    o_in,
    g_in,
    lse_in,
    qn,
    gn,
    rows,
    kv,
    dq,
    own_acc,
    weights,
    gout,
    gin,
    load_sem,
    kv_send,
    kv_recv,
    g_send,
    g_recv,
):
    outer = lax.axis_index("outer")
    inner = lax.axis_index("inner")
    core = lax.rem(inner, 2)
    odd_outer = lax.rem(outer, 2)

    def at(do, di):
        return (lax.rem(outer + do + n_outer, n_outer), lax.rem(inner + di + n_inner, n_inner))

    partner = (outer, inner + 1 - 2 * core)
    senders = [at(0, -2), at(0, -4), at(-1, 0), partner]

    barrier = pltpu.get_barrier_semaphore()
    for sender in senders:
        pl.semaphore_signal(barrier, inc=1, device_id=sender, device_id_type=MESH)

    loads = [
        pltpu.make_async_copy(src, dst, load_sem.at[n])
        for n, (src, dst) in enumerate(
            [
                (g_hbm, g_in),
                (o_hbm, o_in),
                (q_hbm, q_in),
                (lse_hbm, lse_in),
                (k_hbm, kv.at[OWN, 0]),
                (v_hbm, kv.at[OWN, 1]),
            ]
        )
    ]
    for copy in loads:
        copy.start()

    def low_span(block):
        return jnp.minimum(spans[0, block], spans[1, block])

    def is_swapped(block, shape):
        return less(spans[1, block], spans[0, block], shape)

    own_block = outer * n_inner + inner
    own_low = low_span(own_block)
    swapped = is_swapped(own_block, (HALF, DIM))
    swapped_low = narrow(swapped)

    def kv_copies(sources, slot, number, target):
        return [
            pltpu.make_async_remote_copy(
                src_ref=sources[part],
                dst_ref=kv.at[slot, part],
                send_sem=kv_send.at[number, part],
                recv_sem=kv_recv.at[slot, part],
                device_id=target,
                device_id_type=MESH,
            )
            for part in range(2)
        ]

    args = [k_hbm, v_hbm]
    to_four = kv_copies(args, FOUR, 0, at(0, 4))
    on_four = kv_copies([kv.at[TWO, p] for p in range(2)], FOUR, 0, at(0, 2))
    to_two = kv_copies(args, TWO, 1, at(0, 2))
    to_outer = kv_copies(args, OUTER, 2, at(1, 0))
    even_one = kv_copies(args, ONE, 3, partner)
    even_three = kv_copies([kv.at[TWO, p] for p in range(2)], THREE, 4, partner)
    odd_one = kv_copies([kv.at[TWO, p] for p in range(2)], ONE, 3, partner)
    odd_three = kv_copies([kv.at[FOUR, p] for p in range(2)], THREE, 4, partner)

    def received(slot, part):
        pltpu.make_async_remote_copy(
            src_ref=kv.at[slot, part],
            dst_ref=kv.at[slot, part],
            send_sem=kv_send.at[0, part],
            recv_sem=kv_recv.at[slot, part],
            device_id=partner,
            device_id_type=MESH,
        ).wait_recv()

    pl.semaphore_wait(barrier, len(senders))
    for part in range(2):
        to_two[part].start()

        @pl.when(core == 0)
        def _():
            even_one[part].start()

        @pl.when(odd_outer == 1)
        def _():
            to_four[part].start()

    for part in range(2):
        to_outer[part].start()

    for copy in loads:
        copy.wait()
    ones = jnp.ones((8, DIM), jnp.bfloat16)
    for h in range(HEADS):
        col = pl.ds(h * DIM, DIM)
        row = pl.ds(h * HALF, HALF)

        def halves(ref):
            return ordered(swapped_low, ref[pl.ds(0, HALF), col], ref[pl.ds(HALF, HALF), col])

        norms = ordered(swapped[:1], lse_in[h : h + 1, :HALF], lse_in[h : h + 1, HALF:])
        for half, (q, g, o, norm) in enumerate(zip(halves(q_in), halves(g_in), halves(o_in), norms)):
            qn[half, row, :] = q
            gn[half, row, :] = g
            product = g.astype(jnp.float32) * o.astype(jnp.float32)
            top = product.astype(jnp.bfloat16)
            rest = product - top.astype(jnp.float32)
            middle = rest.astype(jnp.bfloat16)
            low = (rest - middle.astype(jnp.float32)).astype(jnp.bfloat16)
            delta = dot(ones, top, NT) + dot(ones, middle, NT) + dot(ones, low, NT)
            rows[half, 0:1, row] = delta[0:1, :]
            rows[half, 1:2, row] = norm * LOG2E

    def attend(keys, q, norm):
        return jnp.exp2(dot(keys, q, NT) * (SCALE * LOG2E) - norm)

    def score_grads(p, values, g, delta):
        return (p * (dot(values, g, NT) - delta)).astype(jnp.bfloat16)

    def halves_of(slot, part, mask):
        return ordered(mask, kv[slot, part, pl.ds(0, HALF), :], kv[slot, part, pl.ds(HALF, HALF), :])

    def own():
        key_at = lax.broadcasted_iota(jnp.int32, (HALF, WIDE), 0)
        query_at = lax.rem(lax.broadcasted_iota(jnp.int32, (HALF, WIDE), 1), HALF)
        seen = key_at <= query_at
        k_lo, k_hi = halves_of(OWN, 0, swapped_low)
        v_lo, v_hi = halves_of(OWN, 1, swapped_low)
        keys = jnp.concatenate([k_lo, k_hi], 0)
        values = jnp.concatenate([v_lo, v_hi], 0)
        p_lo = jnp.where(seen, attend(k_lo, qn[0], rows[0, 1:2, :]), 0.0)
        p_hi = attend(keys, qn[1], rows[1, 1:2, :])
        p_hi = jnp.concatenate([p_hi[:HALF], jnp.where(seen, p_hi[HALF:], 0.0)], 0)
        s_lo = score_grads(p_lo, v_lo, gn[0], rows[0, 0:1, :])
        s_hi = score_grads(p_hi, values, gn[1], rows[1, 0:1, :])
        for part, (lo, hi, other_side) in enumerate(
            [(s_lo, s_hi, qn), (p_lo.astype(jnp.bfloat16), p_hi.astype(jnp.bfloat16), gn)]
        ):
            total = dot(hi, other_side[1], NN)
            first = total[:HALF] + dot(lo, other_side[0], NN)
            own_acc[part, pl.ds(0, HALF), :], own_acc[part, pl.ds(HALF, HALF), :] = ordered(
                swapped, first, total[HALF:]
            )
        dq[:, pl.ds(0, DIM)] = dot(s_lo, k_lo, TN)
        dq[:, pl.ds(DIM, DIM)] = dot(s_hi, keys, TN)

    def sides(do, di):
        there = at(do, di)
        block = there[0] * n_inner + there[1]
        low = low_span(block)
        return (
            less(low, own_low, (HALF, DIM)),
            narrow(less(low, own_low, (WIDE, DIM))),
            less(low, own_low, (1, WIDE)),
            is_swapped(block, (HALF, DIM)),
        )

    def chosen(mask, ref, which):
        other_half = ref[1, which, :] if which is not None else ref[1]
        return jnp.where(mask, ref[0, which, :] if which is not None else ref[0], other_half)

    def put(slot, part, first, second, early, turned):
        lo = first + jnp.where(early, second, 0.0)
        hi = jnp.where(early, 0.0, second)
        for half, value in enumerate(ordered(turned, lo, hi)):
            gout[slot, part, pl.ds(half * HALF, HALF), :] = value.astype(jnp.bfloat16)

    def with_keys(slot, do, di, store):
        early, early_low, early_row, turned = sides(do, di)
        k1, k_hi = halves_of(slot, 0, narrow(turned))
        k2 = jnp.where(early_low[:HALF], k1, k_hi)
        q2 = chosen(early_low, qn, None)
        g2 = chosen(early_low, gn, None)
        norm2 = chosen(early_row, rows, pl.ds(1, 1))
        p1 = attend(k1, qn[1], rows[1, 1:2, :])
        p2 = attend(k2, q2, norm2)
        weights[store, 0] = p1
        weights[store, 1] = p2
        first = dot(p1.astype(jnp.bfloat16), gn[1], NN)
        second = dot(p2.astype(jnp.bfloat16), g2, NN)
        put(slot, 1, first, second, early, turned)

    def with_values(slot, do, di, store):
        early, early_low, early_row, turned = sides(do, di)
        k1, k_hi = halves_of(slot, 0, narrow(turned))
        v1, v_hi = halves_of(slot, 1, narrow(turned))
        k2 = jnp.where(early_low[:HALF], k1, k_hi)
        v2 = jnp.where(early_low[:HALF], v1, v_hi)
        q2 = chosen(early_low, qn, None)
        g2 = chosen(early_low, gn, None)
        delta2 = chosen(early_row, rows, pl.ds(0, 1))
        s1 = score_grads(weights[store, 0], v1, gn[1], rows[1, 0:1, :])
        s2 = score_grads(weights[store, 1], v2, g2, delta2)
        put(slot, 0, dot(s1, qn[1], NN), dot(s2, q2, NN), early, turned)
        zero = jnp.zeros_like(k1)
        wide = jnp.concatenate(
            [
                jnp.concatenate([zero, k1], 1),
                jnp.concatenate(
                    [
                        jnp.where(early_low[:HALF], k2, zero),
                        jnp.where(early_low[:HALF], zero, k2),
                    ],
                    1,
                ),
            ],
            0,
        )
        dq[...] += dot(jnp.concatenate([s1, s2], 0), wide, TN)

    def g_copies(slot, target):
        return [
            pltpu.make_async_remote_copy(
                src_ref=gout.at[slot, part],
                dst_ref=gin.at[slot, part],
                send_sem=g_send.at[slot, part],
                recv_sem=g_recv.at[slot, part],
                device_id=target,
                device_id_type=MESH,
            )
            for part in range(2)
        ]

    g_two = g_copies(TWO, at(0, -2))
    g_four = g_copies(FOUR, at(0, -4))
    g_outer = g_copies(OUTER, at(-1, 0))
    g_one = g_copies(ONE, partner)
    g_three = g_copies(THREE, partner)

    def add_to(slot, extra, part):
        gout[slot, part] = (
            gout[slot, part].astype(jnp.float32) + gin[extra, part].astype(jnp.float32)
        ).astype(jnp.bfloat16)

    def pick(even, odd):
        return even + core * (odd - even)

    def pass_on(part):
        received(TWO, part)

        @pl.when(odd_outer == 0)
        def _():
            on_four[part].start()

        @pl.when(core == 0)
        def _():
            even_three[part].start()

        @pl.when(core == 1)
        def _():
            odd_one[part].start()

    K, V = 0, 1
    own()

    @pl.when(core == 0)
    def _():
        pass_on(K)

    @pl.when(core == 1)
    def _():
        received(ONE, K)

    slot_a, slot_b = pick(TWO, ONE), pick(ONE, TWO)
    with_keys(slot_a, 0, -slot_a, 0)

    @pl.when(core == 0)
    def _():
        received(ONE, K)

    @pl.when(core == 1)
    def _():
        g_one[V].start()
        pass_on(K)

    with_keys(slot_b, 0, -slot_b, 1)

    @pl.when(core == 0)
    def _():
        g_one[V].start()

    @pl.when(core == 1)
    def _():
        received(ONE, V)

    pass_on(V)
    with_values(slot_a, 0, -slot_a, 0)

    @pl.when(core == 0)
    def _():
        received(ONE, V)

    @pl.when(core == 1)
    def _():
        g_one[K].start()

    with_values(slot_b, 0, -slot_b, 1)

    @pl.when(core == 0)
    def _():
        g_one[K].start()

    @pl.when(core == 1)
    def _():
        g_one[V].wait_recv()
        add_to(TWO, ONE, V)
        g_two[V].start()

    slot_c, slot_d = pick(FOUR, THREE), pick(THREE, FOUR)
    received(slot_c, K)
    with_keys(slot_c, 0, -slot_c, 0)

    @pl.when(core == 0)
    def _():
        g_four[V].start()
        received(THREE, K)

    @pl.when(core == 1)
    def _():
        g_three[V].start()
        received(FOUR, K)
        odd_three[K].start()

    with_keys(slot_d, 0, -slot_d, 1)

    @pl.when(core == 0)
    def _():
        g_three[V].start()
        g_three[V].wait_recv()
        add_to(TWO, THREE, V)
        g_two[V].start()

    @pl.when(core == 1)
    def _():
        g_one[K].wait_recv()
        add_to(TWO, ONE, K)
        g_two[K].start()

    received(slot_c, V)
    with_values(slot_c, 0, -slot_c, 0)

    @pl.when(core == 0)
    def _():
        g_four[K].start()
        received(THREE, V)

    @pl.when(core == 1)
    def _():
        g_three[K].start()
        received(FOUR, V)
        odd_three[V].start()

    with_values(slot_d, 0, -slot_d, 1)

    @pl.when(core == 0)
    def _():
        g_three[K].start()
        g_three[K].wait_recv()
        add_to(TWO, THREE, K)
        g_two[K].start()

    @pl.when(core == 1)
    def _():
        g_three[V].wait_recv()
        add_to(FOUR, THREE, V)
        g_four[V].start()

    received(OUTER, K)
    with_keys(OUTER, -1, 0, 0)
    g_outer[V].start()
    received(OUTER, V)
    with_values(OUTER, -1, 0, 0)
    g_outer[K].start()

    @pl.when(core == 1)
    def _():
        g_three[K].wait_recv()
        add_to(FOUR, THREE, K)
        g_four[K].start()

    for h in range(HEADS):
        row = pl.ds(h * HALF, HALF)
        col = pl.ds(h * DIM, DIM)
        first, second = ordered(swapped, dq[row, pl.ds(0, DIM)], dq[row, pl.ds(DIM, DIM)])
        dq_out[pl.ds(0, HALF), col] = first * SCALE
        dq_out[pl.ds(HALF, HALF), col] = second * SCALE

    @pl.when(core == 0)
    def _():
        for part in range(2):
            g_one[part].wait_recv()
            own_acc[part] += gin[ONE, part].astype(jnp.float32)

    for part, out, factor in [(V, dv_out, 1.0), (K, dk_out, SCALE)]:
        total = own_acc[part]
        for slot, copies in [(TWO, g_two), (OUTER, g_outer), (FOUR, g_four)]:
            copies[part].wait_recv()
            total = total + gin[slot, part].astype(jnp.float32)
        out[...] = total * factor
    for copies in (to_four, to_two, to_outer, odd_one, odd_three):
        for copy in copies:
            copy.wait_send()
    for copies in (g_two, g_four, g_outer, g_one, g_three):
        for copy in copies:
            copy.wait_send()


def write_out(*refs):
    sources, results, sem = refs[:3], refs[3:6], refs[6]
    copies = [
        pltpu.make_async_copy(src, dst, sem.at[n])
        for n, (src, dst) in enumerate(zip(sources, results))
    ]
    for copy in copies:
        copy.start()
    for copy in copies:
        copy.wait()


def local(n_outer, n_inner, queries, keys, values, outputs, out_grads, log_sum_exp, span_ids):
    block, dim = keys.shape
    width = queries.shape[1]
    heads = log_sum_exp.shape[0]
    bf16, f32 = jnp.bfloat16, jnp.float32
    in_hbm = pl.BlockSpec(memory_space=pltpu.HBM)
    in_vmem = pl.BlockSpec(memory_space=pltpu.VMEM)
    arrays = [
        pltpu.with_memory_space_constraint(a, pltpu.HBM)
        for a in (queries, keys, values, outputs, out_grads, log_sum_exp)
    ]
    shapes = [(block, width), (block, dim), (block, dim)]
    grads = pl.pallas_call(
        functools.partial(kernel, n_outer, n_inner),
        out_shape=tuple(pltpu.VMEM(shape, f32) for shape in shapes),
        in_specs=[pl.BlockSpec(memory_space=pltpu.SMEM)] + [in_hbm] * 6,
        out_specs=(in_vmem,) * 3,
        scratch_shapes=[
            pltpu.VMEM((block, width), bf16),
            pltpu.VMEM((block, width), bf16),
            pltpu.VMEM((block, width), bf16),
            pltpu.VMEM((heads, block), f32),
            pltpu.VMEM((2, heads * HALF, dim), bf16),
            pltpu.VMEM((2, heads * HALF, dim), bf16),
            pltpu.VMEM((2, 8, heads * HALF), f32),
            pltpu.VMEM((6, 2, block, dim), bf16),
            pltpu.VMEM((heads * HALF, 2 * dim), f32),
            pltpu.VMEM((2, block, dim), f32),
            pltpu.VMEM((2, 2, HALF, heads * HALF), f32),
            pltpu.VMEM((6, 2, block, dim), bf16),
            pltpu.VMEM((6, 2, block, dim), bf16),
            pltpu.SemaphoreType.DMA((6,)),
            pltpu.SemaphoreType.DMA((5, 2)),
            pltpu.SemaphoreType.DMA((6, 2)),
            pltpu.SemaphoreType.DMA((6, 2)),
            pltpu.SemaphoreType.DMA((6, 2)),
        ],
        compiler_params=pltpu.CompilerParams(
            collective_id=0, has_side_effects=True, vmem_limit_bytes=48 * 1024 * 1024
        ),
        name="backward",
    )(pltpu.with_memory_space_constraint(span_ids, pltpu.HBM), *arrays)
    return pl.pallas_call(
        write_out,
        out_shape=tuple(jax.ShapeDtypeStruct(shape, f32) for shape in shapes),
        in_specs=[in_vmem] * 3,
        out_specs=(pl.BlockSpec(memory_space=pl.ANY),) * 3,
        scratch_shapes=[pltpu.SemaphoreType.DMA((3,))],
        name="write_out",
    )(*(pltpu.with_memory_space_constraint(a, pltpu.VMEM) for a in grads))


def solution(mesh):
    tokens = P(("outer", "inner"), None)
    return jax.shard_map(
        functools.partial(local, mesh.shape["outer"], mesh.shape["inner"]),
        mesh=mesh,
        in_specs=(tokens,) * 5 + (P(None, ("outer", "inner")), P()),
        out_specs=(tokens,) * 3,
        check_vma=False,
    )
```

```python
import functools
import math

import jax
import jax.numpy as jnp
from jax import lax
from jax.experimental import pallas as pl
from jax.experimental.pallas import tpu as pltpu
from jax.sharding import PartitionSpec as P

MESH = pl.DeviceIdType.MESH
HALF = 128
DIM = 128
HEADS = 8
WIDE = HEADS * HALF
NT = (((1,), (1,)), ((), ()))
NN = (((1,), (0,)), ((), ()))
TN = (((0,), (0,)), ((), ()))
LOG2E = math.log2(math.e)
SCALE = DIM ** (-0.5)

OWN, ONE, TWO, THREE, FOUR, OUTER = range(6)


def dot(a, b, dims):
    return lax.dot_general(a, b, dims, preferred_element_type=jnp.float32)


def less(a, b, shape):
    return jnp.full(shape, a, jnp.int32) < jnp.full(shape, b, jnp.int32)


def narrow(mask):
    return jnp.where(mask, 1.0, 0.0).astype(jnp.bfloat16) > 0.5


def ordered(swapped, first, second):
    return jnp.where(swapped, second, first), jnp.where(swapped, first, second)


def kernel(
    n_outer,
    n_inner,
    spans_hbm,
    q_hbm,
    k_hbm,
    v_hbm,
    o_hbm,
    g_hbm,
    lse_hbm,
    dq_out,
    dk_out,
    dv_out,
    spans,
    q_in,
    o_in,
    g_in,
    lse_in,
    qn,
    gn,
    rows,
    kv,
    dq,
    own_acc,
    weights,
    gout,
    gin,
    load_sem,
    kv_send,
    kv_recv,
    g_send,
    g_recv,
):
    outer = lax.axis_index("outer")
    inner = lax.axis_index("inner")
    core = lax.rem(inner, 2)
    odd_outer = lax.rem(outer, 2)

    def at(do, di):
        return (lax.rem(outer + do + n_outer, n_outer), lax.rem(inner + di + n_inner, n_inner))

    partner = (outer, inner + 1 - 2 * core)
    senders = [at(0, -2), at(0, -4), at(-1, 0), partner]

    barrier = pltpu.get_barrier_semaphore()
    for sender in senders:
        pl.semaphore_signal(barrier, inc=1, device_id=sender, device_id_type=MESH)

    loads = [
        pltpu.make_async_copy(src, dst, load_sem.at[n])
        for n, (src, dst) in enumerate(
            [
                (g_hbm, g_in),
                (o_hbm, o_in),
                (q_hbm, q_in),
                (lse_hbm, lse_in),
                (k_hbm, kv.at[OWN, 0]),
                (v_hbm, kv.at[OWN, 1]),
                (spans_hbm, spans),
            ]
        )
    ]
    for copy in loads:
        copy.start()

    def low_span(block):
        return jnp.minimum(spans[0, block], spans[1, block])

    def is_swapped(block, shape):
        return less(spans[1, block], spans[0, block], shape)

    def kv_copies(sources, slot, number, target):
        return [
            pltpu.make_async_remote_copy(
                src_ref=sources[part],
                dst_ref=kv.at[slot, part],
                send_sem=kv_send.at[number, part],
                recv_sem=kv_recv.at[slot, part],
                device_id=target,
                device_id_type=MESH,
            )
            for part in range(2)
        ]

    args = [k_hbm, v_hbm]
    to_four = kv_copies(args, FOUR, 0, at(0, 4))
    on_four = kv_copies([kv.at[TWO, p] for p in range(2)], FOUR, 0, at(0, 2))
    to_two = kv_copies(args, TWO, 1, at(0, 2))
    to_outer = kv_copies(args, OUTER, 2, at(1, 0))
    even_one = kv_copies(args, ONE, 3, partner)
    even_three = kv_copies([kv.at[TWO, p] for p in range(2)], THREE, 4, partner)
    odd_one = kv_copies([kv.at[TWO, p] for p in range(2)], ONE, 3, partner)
    odd_three = kv_copies([kv.at[FOUR, p] for p in range(2)], THREE, 4, partner)

    def received(slot, part):
        pltpu.make_async_remote_copy(
            src_ref=kv.at[slot, part],
            dst_ref=kv.at[slot, part],
            send_sem=kv_send.at[0, part],
            recv_sem=kv_recv.at[slot, part],
            device_id=partner,
            device_id_type=MESH,
        ).wait_recv()

    pl.semaphore_wait(barrier, len(senders))
    for part in range(2):
        to_two[part].start()

        @pl.when(core == 0)
        def _():
            even_one[part].start()

        @pl.when(odd_outer == 1)
        def _():
            to_four[part].start()

    for part in range(2):
        to_outer[part].start()

    for copy in loads:
        copy.wait()
    own_block = outer * n_inner + inner
    own_low = low_span(own_block)
    swapped = is_swapped(own_block, (HALF, DIM))
    swapped_low = narrow(swapped)
    ones = jnp.ones((8, DIM), jnp.bfloat16)
    for h in range(HEADS):
        col = pl.ds(h * DIM, DIM)
        row = pl.ds(h * HALF, HALF)

        def halves(ref):
            return ordered(swapped_low, ref[pl.ds(0, HALF), col], ref[pl.ds(HALF, HALF), col])

        norms = ordered(swapped[:1], lse_in[h : h + 1, :HALF], lse_in[h : h + 1, HALF:])
        for half, (q, g, o, norm) in enumerate(zip(halves(q_in), halves(g_in), halves(o_in), norms)):
            qn[half, row, :] = q
            gn[half, row, :] = g
            product = g.astype(jnp.float32) * o.astype(jnp.float32)
            top = product.astype(jnp.bfloat16)
            rest = product - top.astype(jnp.float32)
            middle = rest.astype(jnp.bfloat16)
            low = (rest - middle.astype(jnp.float32)).astype(jnp.bfloat16)
            delta = dot(ones, top, NT) + dot(ones, middle, NT) + dot(ones, low, NT)
            rows[half, 0:1, row] = delta[0:1, :]
            rows[half, 1:2, row] = norm * LOG2E

    def attend(keys, q, norm):
        return jnp.exp2(dot(keys, q, NT) * (SCALE * LOG2E) - norm)

    def score_grads(p, values, g, delta):
        return (p * (dot(values, g, NT) - delta)).astype(jnp.bfloat16)

    def halves_of(slot, part, mask):
        return ordered(mask, kv[slot, part, pl.ds(0, HALF), :], kv[slot, part, pl.ds(HALF, HALF), :])

    def own():
        key_at = lax.broadcasted_iota(jnp.int32, (HALF, WIDE), 0)
        query_at = lax.rem(lax.broadcasted_iota(jnp.int32, (HALF, WIDE), 1), HALF)
        seen = key_at <= query_at
        k_lo, k_hi = halves_of(OWN, 0, swapped_low)
        v_lo, v_hi = halves_of(OWN, 1, swapped_low)
        keys = jnp.concatenate([k_lo, k_hi], 0)
        values = jnp.concatenate([v_lo, v_hi], 0)
        p_lo = jnp.where(seen, attend(k_lo, qn[0], rows[0, 1:2, :]), 0.0)
        p_hi = attend(keys, qn[1], rows[1, 1:2, :])
        p_hi = jnp.concatenate([p_hi[:HALF], jnp.where(seen, p_hi[HALF:], 0.0)], 0)
        s_lo = score_grads(p_lo, v_lo, gn[0], rows[0, 0:1, :])
        s_hi = score_grads(p_hi, values, gn[1], rows[1, 0:1, :])
        for part, (lo, hi, other_side) in enumerate(
            [(s_lo, s_hi, qn), (p_lo.astype(jnp.bfloat16), p_hi.astype(jnp.bfloat16), gn)]
        ):
            total = dot(hi, other_side[1], NN)
            first = total[:HALF] + dot(lo, other_side[0], NN)
            own_acc[part, pl.ds(0, HALF), :], own_acc[part, pl.ds(HALF, HALF), :] = ordered(
                swapped, first, total[HALF:]
            )
        dq[:, pl.ds(0, DIM)] = dot(s_lo, k_lo, TN)
        dq[:, pl.ds(DIM, DIM)] = dot(s_hi, keys, TN)

    def sides(do, di):
        there = at(do, di)
        block = there[0] * n_inner + there[1]
        low = low_span(block)
        return (
            less(low, own_low, (HALF, DIM)),
            narrow(less(low, own_low, (WIDE, DIM))),
            less(low, own_low, (1, WIDE)),
            is_swapped(block, (HALF, DIM)),
        )

    def chosen(mask, ref, which):
        other_half = ref[1, which, :] if which is not None else ref[1]
        return jnp.where(mask, ref[0, which, :] if which is not None else ref[0], other_half)

    def put(slot, part, first, second, early, turned):
        lo = first + jnp.where(early, second, 0.0)
        hi = jnp.where(early, 0.0, second)
        for half, value in enumerate(ordered(turned, lo, hi)):
            gout[slot, part, pl.ds(half * HALF, HALF), :] = value.astype(jnp.bfloat16)

    def with_keys(slot, do, di, store):
        early, early_low, early_row, turned = sides(do, di)
        k1, k_hi = halves_of(slot, 0, narrow(turned))
        k2 = jnp.where(early_low[:HALF], k1, k_hi)
        q2 = chosen(early_low, qn, None)
        g2 = chosen(early_low, gn, None)
        norm2 = chosen(early_row, rows, pl.ds(1, 1))
        p1 = attend(k1, qn[1], rows[1, 1:2, :])
        p2 = attend(k2, q2, norm2)
        weights[store, 0] = p1
        weights[store, 1] = p2
        first = dot(p1.astype(jnp.bfloat16), gn[1], NN)
        second = dot(p2.astype(jnp.bfloat16), g2, NN)
        put(slot, 1, first, second, early, turned)

    def with_values(slot, do, di, store):
        early, early_low, early_row, turned = sides(do, di)
        k1, k_hi = halves_of(slot, 0, narrow(turned))
        v1, v_hi = halves_of(slot, 1, narrow(turned))
        k2 = jnp.where(early_low[:HALF], k1, k_hi)
        v2 = jnp.where(early_low[:HALF], v1, v_hi)
        q2 = chosen(early_low, qn, None)
        g2 = chosen(early_low, gn, None)
        delta2 = chosen(early_row, rows, pl.ds(0, 1))
        s1 = score_grads(weights[store, 0], v1, gn[1], rows[1, 0:1, :])
        s2 = score_grads(weights[store, 1], v2, g2, delta2)
        put(slot, 0, dot(s1, qn[1], NN), dot(s2, q2, NN), early, turned)
        zero = jnp.zeros_like(k1)
        wide = jnp.concatenate(
            [
                jnp.concatenate([zero, k1], 1),
                jnp.concatenate(
                    [
                        jnp.where(early_low[:HALF], k2, zero),
                        jnp.where(early_low[:HALF], zero, k2),
                    ],
                    1,
                ),
            ],
            0,
        )
        dq[...] += dot(jnp.concatenate([s1, s2], 0), wide, TN)

    def g_copies(slot, target):
        return [
            pltpu.make_async_remote_copy(
                src_ref=gout.at[slot, part],
                dst_ref=gin.at[slot, part],
                send_sem=g_send.at[slot, part],
                recv_sem=g_recv.at[slot, part],
                device_id=target,
                device_id_type=MESH,
            )
            for part in range(2)
        ]

    g_two = g_copies(TWO, at(0, -2))
    g_four = g_copies(FOUR, at(0, -4 + 2 * odd_outer))
    g_outer = g_copies(OUTER, at(-1, 0))
    g_one = g_copies(ONE, partner)
    g_three = g_copies(THREE, partner)

    def add_to(slot, extra, part):
        gout[slot, part] = (
            gout[slot, part].astype(jnp.float32) + gin[extra, part].astype(jnp.float32)
        ).astype(jnp.bfloat16)

    def pick(even, odd):
        return even + core * (odd - even)

    def pass_on(part):
        received(TWO, part)

        @pl.when(odd_outer == 0)
        def _():
            on_four[part].start()

        @pl.when(core == 0)
        def _():
            even_three[part].start()

        @pl.when(core == 1)
        def _():
            odd_one[part].start()

    K, V = 0, 1

    def merge(copies, slot, extra, arrived, part):
        arrived[part].wait_recv()
        add_to(slot, extra, part)
        if copies is not None:
            copies[part].start()

    def send_two(part):
        @pl.when(odd_outer == 0)
        def _():
            g_two[part].start()

    own()

    @pl.when(core == 0)
    def _():
        pass_on(K)

    @pl.when(core == 1)
    def _():
        received(ONE, K)

    slot_a, slot_b = pick(TWO, ONE), pick(ONE, TWO)
    with_keys(slot_a, 0, -slot_a, 0)

    @pl.when(core == 0)
    def _():
        received(ONE, K)

    @pl.when(core == 1)
    def _():
        g_one[V].start()
        pass_on(K)

    with_keys(slot_b, 0, -slot_b, 1)

    @pl.when(core == 0)
    def _():
        g_one[V].start()

    @pl.when(core == 1)
    def _():
        received(ONE, V)

    pass_on(V)
    with_values(slot_a, 0, -slot_a, 0)

    @pl.when(core == 0)
    def _():
        received(ONE, V)

    @pl.when(core == 1)
    def _():
        g_one[K].start()

    with_values(slot_b, 0, -slot_b, 1)

    @pl.when(core == 0)
    def _():
        g_one[K].start()

    @pl.when(core == 1)
    def _():
        received(THREE, K)
        with_keys(THREE, 0, -THREE, 0)
        g_three[V].start()
        merge(None, TWO, ONE, g_one, V)
        send_two(V)
        received(THREE, V)
        with_values(THREE, 0, -THREE, 0)
        g_three[K].start()
        merge(None, TWO, ONE, g_one, K)
        send_two(K)


    @pl.when(core == 0)
    def _():
        merge(None, TWO, THREE, g_three, V)
        send_two(V)
        merge(None, TWO, THREE, g_three, K)
        send_two(K)

        received(FOUR, K)
        with_keys(FOUR, 0, -FOUR, 0)
        g_four[V].start()
        received(THREE, K)
        with_keys(THREE, 0, -THREE, 1)
        g_three[V].start()
        received(FOUR, V)
        with_values(FOUR, 0, -FOUR, 0)
        g_four[K].start()
        received(THREE, V)
        with_values(THREE, 0, -THREE, 1)
        g_three[K].start()

    @pl.when(core == 1)
    def _():
        received(FOUR, K)
        odd_three[K].start()
        with_keys(FOUR, 0, -FOUR, 0)
        received(FOUR, V)
        odd_three[V].start()
        with_values(FOUR, 0, -FOUR, 0)
        merge(g_four, FOUR, THREE, g_three, V)
        merge(g_four, FOUR, THREE, g_three, K)

    received(OUTER, K)
    with_keys(OUTER, -1, 0, 0)
    g_outer[V].start()
    received(OUTER, V)
    with_values(OUTER, -1, 0, 0)
    g_outer[K].start()


    @pl.when(odd_outer == 1)
    def _():
        merge(g_two, TWO, FOUR, g_four, V)
        merge(g_two, TWO, FOUR, g_four, K)

    for h in range(HEADS):
        row = pl.ds(h * HALF, HALF)
        col = pl.ds(h * DIM, DIM)
        first, second = ordered(swapped, dq[row, pl.ds(0, DIM)], dq[row, pl.ds(DIM, DIM)])
        dq_out[pl.ds(0, HALF), col] = first * SCALE
        dq_out[pl.ds(HALF, HALF), col] = second * SCALE

    @pl.when(core == 0)
    def _():
        for part in range(2):
            g_one[part].wait_recv()
            own_acc[part] += gin[ONE, part].astype(jnp.float32)

    for part, out, factor in [(V, dv_out, 1.0), (K, dk_out, SCALE)]:
        total = own_acc[part]
        for slot, copies in [(OUTER, g_outer), (TWO, g_two)]:
            copies[part].wait_recv()
            total = total + gin[slot, part].astype(jnp.float32)
        own_acc[part] = total

        @pl.when(odd_outer == 0)
        def _():
            g_four[part].wait_recv()
            own_acc[part] += gin[FOUR, part].astype(jnp.float32)

        out[...] = own_acc[part] * factor
    for copies in (to_four, to_two, to_outer, odd_one, odd_three):
        for copy in copies:
            copy.wait_send()
    for copies in (g_two, g_four, g_outer, g_one, g_three):
        for copy in copies:
            copy.wait_send()


def write_out(*refs):
    sources, results, sem = refs[:3], refs[3:6], refs[6]
    copies = [
        pltpu.make_async_copy(src, dst, sem.at[n])
        for n, (src, dst) in enumerate(zip(sources, results))
    ]
    for copy in copies:
        copy.start()
    for copy in copies:
        copy.wait()


def local(n_outer, n_inner, queries, keys, values, outputs, out_grads, log_sum_exp, span_ids):
    block, dim = keys.shape
    width = queries.shape[1]
    heads = log_sum_exp.shape[0]
    bf16, f32 = jnp.bfloat16, jnp.float32
    in_hbm = pl.BlockSpec(memory_space=pltpu.HBM)
    in_vmem = pl.BlockSpec(memory_space=pltpu.VMEM)
    arrays = [
        pltpu.with_memory_space_constraint(a, pltpu.HBM)
        for a in (queries, keys, values, outputs, out_grads, log_sum_exp)
    ]
    shapes = [(block, width), (block, dim), (block, dim)]
    grads = pl.pallas_call(
        functools.partial(kernel, n_outer, n_inner),
        out_shape=tuple(pltpu.VMEM(shape, f32) for shape in shapes),
        in_specs=[in_hbm] * 7,
        out_specs=(in_vmem,) * 3,
        scratch_shapes=[
            pltpu.SMEM(span_ids.shape, jnp.int32),
            pltpu.VMEM((block, width), bf16),
            pltpu.VMEM((block, width), bf16),
            pltpu.VMEM((block, width), bf16),
            pltpu.VMEM((heads, block), f32),
            pltpu.VMEM((2, heads * HALF, dim), bf16),
            pltpu.VMEM((2, heads * HALF, dim), bf16),
            pltpu.VMEM((2, 8, heads * HALF), f32),
            pltpu.VMEM((6, 2, block, dim), bf16),
            pltpu.VMEM((heads * HALF, 2 * dim), f32),
            pltpu.VMEM((2, block, dim), f32),
            pltpu.VMEM((2, 2, HALF, heads * HALF), f32),
            pltpu.VMEM((6, 2, block, dim), bf16),
            pltpu.VMEM((6, 2, block, dim), bf16),
            pltpu.SemaphoreType.DMA((7,)),
            pltpu.SemaphoreType.DMA((5, 2)),
            pltpu.SemaphoreType.DMA((6, 2)),
            pltpu.SemaphoreType.DMA((6, 2)),
            pltpu.SemaphoreType.DMA((6, 2)),
        ],
        compiler_params=pltpu.CompilerParams(
            collective_id=0, has_side_effects=True, vmem_limit_bytes=48 * 1024 * 1024
        ),
        name="backward",
    )(pltpu.with_memory_space_constraint(span_ids, pltpu.HBM), *arrays)
    return pl.pallas_call(
        write_out,
        out_shape=tuple(jax.ShapeDtypeStruct(shape, f32) for shape in shapes),
        in_specs=[in_vmem] * 3,
        out_specs=(pl.BlockSpec(memory_space=pl.ANY),) * 3,
        scratch_shapes=[pltpu.SemaphoreType.DMA((3,))],
        name="write_out",
    )(*(pltpu.with_memory_space_constraint(a, pltpu.VMEM) for a in grads))


def solution(mesh):
    tokens = P(("outer", "inner"), None)
    return jax.shard_map(
        functools.partial(local, mesh.shape["outer"], mesh.shape["inner"]),
        mesh=mesh,
        in_specs=(tokens,) * 5 + (P(None, ("outer", "inner")), P()),
        out_specs=(tokens,) * 3,
        check_vma=False,
    )
```

```python
import functools
import math

import jax
import jax.numpy as jnp
from jax import lax
from jax.experimental import pallas as pl
from jax.experimental.pallas import tpu as pltpu
from jax.sharding import PartitionSpec as P

MESH = pl.DeviceIdType.MESH
HALF = 128
DIM = 128
HEADS = 8
WIDE = HEADS * HALF
NT = (((1,), (1,)), ((), ()))
NN = (((1,), (0,)), ((), ()))
TN = (((0,), (0,)), ((), ()))
LOG2E = math.log2(math.e)
SCALE = DIM ** (-0.5)

OWN, ONE, TWO, THREE, FOUR, OUTER = range(6)


def dot(a, b, dims):
    return lax.dot_general(a, b, dims, preferred_element_type=jnp.float32)


def less(a, b, shape):
    return jnp.full(shape, a, jnp.int32) < jnp.full(shape, b, jnp.int32)


def narrow(mask):
    return jnp.where(mask, 1.0, 0.0).astype(jnp.bfloat16) > 0.5


def ordered(swapped, first, second):
    return jnp.where(swapped, second, first), jnp.where(swapped, first, second)


def kernel(
    n_outer,
    n_inner,
    spans_hbm,
    q_hbm,
    k_hbm,
    v_hbm,
    o_hbm,
    g_hbm,
    lse_hbm,
    dq_out,
    dk_out,
    dv_out,
    spans,
    q_in,
    o_in,
    g_in,
    lse_in,
    qn,
    gn,
    rows,
    kv,
    dq,
    own_acc,
    weights,
    gout,
    gin,
    load_sem,
    kv_send,
    kv_recv,
    g_send,
    g_recv,
):
    outer = lax.axis_index("outer")
    inner = lax.axis_index("inner")
    core = lax.rem(inner, 2)
    odd_outer = lax.rem(outer, 2)

    def at(do, di):
        return (lax.rem(outer + do + n_outer, n_outer), lax.rem(inner + di + n_inner, n_inner))

    partner = (outer, inner + 1 - 2 * core)
    senders = [at(0, -2), at(0, -4), at(-1, 0), partner]

    barrier = pltpu.get_barrier_semaphore()
    for sender in senders:
        pl.semaphore_signal(barrier, inc=1, device_id=sender, device_id_type=MESH)

    loads = [
        pltpu.make_async_copy(src, dst, load_sem.at[n])
        for n, (src, dst) in enumerate(
            [
                (g_hbm, g_in),
                (o_hbm, o_in),
                (q_hbm, q_in),
                (lse_hbm, lse_in),
                (k_hbm, kv.at[OWN, 0]),
                (v_hbm, kv.at[OWN, 1]),
                (spans_hbm, spans),
            ]
        )
    ]
    for copy in loads:
        copy.start()

    def low_span(block):
        return jnp.minimum(spans[0, block], spans[1, block])

    def is_swapped(block, shape):
        return less(spans[1, block], spans[0, block], shape)

    def kv_copies(sources, slot, number, target):
        return [
            pltpu.make_async_remote_copy(
                src_ref=sources[part],
                dst_ref=kv.at[slot, part],
                send_sem=kv_send.at[number, part],
                recv_sem=kv_recv.at[slot, part],
                device_id=target,
                device_id_type=MESH,
            )
            for part in range(2)
        ]

    args = [k_hbm, v_hbm]
    to_four = kv_copies(args, FOUR, 0, at(0, 4))
    on_four = kv_copies([kv.at[TWO, p] for p in range(2)], FOUR, 0, at(0, 2))
    to_two = kv_copies(args, TWO, 1, at(0, 2))
    to_outer = kv_copies(args, OUTER, 2, at(1, 0))
    even_one = kv_copies(args, ONE, 3, partner)
    even_three = kv_copies([kv.at[TWO, p] for p in range(2)], THREE, 4, partner)
    odd_one = kv_copies([kv.at[TWO, p] for p in range(2)], ONE, 3, partner)
    odd_three = kv_copies([kv.at[FOUR, p] for p in range(2)], THREE, 4, partner)

    def received(slot, part):
        pltpu.make_async_remote_copy(
            src_ref=kv.at[slot, part],
            dst_ref=kv.at[slot, part],
            send_sem=kv_send.at[0, part],
            recv_sem=kv_recv.at[slot, part],
            device_id=partner,
            device_id_type=MESH,
        ).wait_recv()

    pl.semaphore_wait(barrier, len(senders))
    for part in range(2):
        to_two[part].start()

        @pl.when(core == 0)
        def _():
            even_one[part].start()

        @pl.when(odd_outer == 1)
        def _():
            to_four[part].start()

    @pl.when(odd_outer == 1)
    def _():
        for part in range(2):
            to_outer[part].start()

    for copy in loads:
        copy.wait()
    own_block = outer * n_inner + inner
    own_low = low_span(own_block)
    swapped = is_swapped(own_block, (HALF, DIM))
    swapped_low = narrow(swapped)
    ones = jnp.ones((8, DIM), jnp.bfloat16)
    for h in range(HEADS):
        col = pl.ds(h * DIM, DIM)
        row = pl.ds(h * HALF, HALF)

        def halves(ref):
            return ordered(swapped_low, ref[pl.ds(0, HALF), col], ref[pl.ds(HALF, HALF), col])

        norms = ordered(swapped[:1], lse_in[h : h + 1, :HALF], lse_in[h : h + 1, HALF:])
        for half, (q, g, o, norm) in enumerate(zip(halves(q_in), halves(g_in), halves(o_in), norms)):
            qn[half, row, :] = q
            gn[half, row, :] = g
            product = g.astype(jnp.float32) * o.astype(jnp.float32)
            top = product.astype(jnp.bfloat16)
            rest = product - top.astype(jnp.float32)
            middle = rest.astype(jnp.bfloat16)
            low = (rest - middle.astype(jnp.float32)).astype(jnp.bfloat16)
            delta = dot(ones, top, NT) + dot(ones, middle, NT) + dot(ones, low, NT)
            rows[half, 0:1, row] = delta[0:1, :]
            rows[half, 1:2, row] = norm * LOG2E

    def attend(keys, q, norm):
        return jnp.exp2(dot(keys, q, NT) * (SCALE * LOG2E) - norm)

    def score_grads(p, values, g, delta):
        return (p * (dot(values, g, NT) - delta)).astype(jnp.bfloat16)

    def halves_of(slot, part, mask):
        return ordered(mask, kv[slot, part, pl.ds(0, HALF), :], kv[slot, part, pl.ds(HALF, HALF), :])

    def own():
        key_at = lax.broadcasted_iota(jnp.int32, (HALF, WIDE), 0)
        query_at = lax.rem(lax.broadcasted_iota(jnp.int32, (HALF, WIDE), 1), HALF)
        seen = key_at <= query_at
        k_lo, k_hi = halves_of(OWN, 0, swapped_low)
        v_lo, v_hi = halves_of(OWN, 1, swapped_low)
        keys = jnp.concatenate([k_lo, k_hi], 0)
        values = jnp.concatenate([v_lo, v_hi], 0)
        p_lo = jnp.where(seen, attend(k_lo, qn[0], rows[0, 1:2, :]), 0.0)
        p_hi = attend(keys, qn[1], rows[1, 1:2, :])
        p_hi = jnp.concatenate([p_hi[:HALF], jnp.where(seen, p_hi[HALF:], 0.0)], 0)
        s_lo = score_grads(p_lo, v_lo, gn[0], rows[0, 0:1, :])
        s_hi = score_grads(p_hi, values, gn[1], rows[1, 0:1, :])
        for part, (lo, hi, other_side) in enumerate(
            [(s_lo, s_hi, qn), (p_lo.astype(jnp.bfloat16), p_hi.astype(jnp.bfloat16), gn)]
        ):
            total = dot(hi, other_side[1], NN)
            first = total[:HALF] + dot(lo, other_side[0], NN)
            own_acc[part, pl.ds(0, HALF), :], own_acc[part, pl.ds(HALF, HALF), :] = ordered(
                swapped, first, total[HALF:]
            )
        dq[:, pl.ds(0, DIM)] = dot(s_lo, k_lo, TN)
        dq[:, pl.ds(DIM, DIM)] = dot(s_hi, keys, TN)

    def sides(do, di):
        there = at(do, di)
        block = there[0] * n_inner + there[1]
        low = low_span(block)
        return (
            less(low, own_low, (HALF, DIM)),
            narrow(less(low, own_low, (WIDE, DIM))),
            less(low, own_low, (1, WIDE)),
            is_swapped(block, (HALF, DIM)),
        )

    def chosen(mask, ref, which):
        other_half = ref[1, which, :] if which is not None else ref[1]
        return jnp.where(mask, ref[0, which, :] if which is not None else ref[0], other_half)

    def put(slot, part, first, second, early, turned):
        lo = first + jnp.where(early, second, 0.0)
        hi = jnp.where(early, 0.0, second)
        for half, value in enumerate(ordered(turned, lo, hi)):
            gout[slot, part, pl.ds(half * HALF, HALF), :] = value.astype(jnp.bfloat16)

    def with_keys(slot, do, di, store):
        early, early_low, early_row, turned = sides(do, di)
        k1, k_hi = halves_of(slot, 0, narrow(turned))
        k2 = jnp.where(early_low[:HALF], k1, k_hi)
        q2 = chosen(early_low, qn, None)
        g2 = chosen(early_low, gn, None)
        norm2 = chosen(early_row, rows, pl.ds(1, 1))
        p1 = attend(k1, qn[1], rows[1, 1:2, :])
        p2 = attend(k2, q2, norm2)
        weights[store, 0] = p1
        weights[store, 1] = p2
        first = dot(p1.astype(jnp.bfloat16), gn[1], NN)
        second = dot(p2.astype(jnp.bfloat16), g2, NN)
        put(slot, 1, first, second, early, turned)

    def with_values(slot, do, di, store):
        early, early_low, early_row, turned = sides(do, di)
        k1, k_hi = halves_of(slot, 0, narrow(turned))
        v1, v_hi = halves_of(slot, 1, narrow(turned))
        k2 = jnp.where(early_low[:HALF], k1, k_hi)
        v2 = jnp.where(early_low[:HALF], v1, v_hi)
        q2 = chosen(early_low, qn, None)
        g2 = chosen(early_low, gn, None)
        delta2 = chosen(early_row, rows, pl.ds(0, 1))
        s1 = score_grads(weights[store, 0], v1, gn[1], rows[1, 0:1, :])
        s2 = score_grads(weights[store, 1], v2, g2, delta2)
        put(slot, 0, dot(s1, qn[1], NN), dot(s2, q2, NN), early, turned)
        zero = jnp.zeros_like(k1)
        wide = jnp.concatenate(
            [
                jnp.concatenate([zero, k1], 1),
                jnp.concatenate(
                    [
                        jnp.where(early_low[:HALF], k2, zero),
                        jnp.where(early_low[:HALF], zero, k2),
                    ],
                    1,
                ),
            ],
            0,
        )
        dq[...] += dot(jnp.concatenate([s1, s2], 0), wide, TN)

    def g_copies(slot, target):
        return [
            pltpu.make_async_remote_copy(
                src_ref=gout.at[slot, part],
                dst_ref=gin.at[slot, part],
                send_sem=g_send.at[slot, part],
                recv_sem=g_recv.at[slot, part],
                device_id=target,
                device_id_type=MESH,
            )
            for part in range(2)
        ]

    g_two = g_copies(TWO, at(0, -2))
    g_four = g_copies(FOUR, at(0, -4 + 2 * odd_outer))
    g_outer = g_copies(OUTER, at(-1, 0))
    g_one = g_copies(ONE, partner)
    g_three = g_copies(THREE, partner)

    def add_to(slot, extra, part):
        gout[slot, part] = (
            gout[slot, part].astype(jnp.float32) + gin[extra, part].astype(jnp.float32)
        ).astype(jnp.bfloat16)

    def pick(even, odd):
        return even + core * (odd - even)

    def pass_on(part):
        received(TWO, part)

        @pl.when(odd_outer == 0)
        def _():
            on_four[part].start()
            if part == 0:
                to_outer[0].start()
                to_outer[1].start()

        @pl.when(core == 0)
        def _():
            even_three[part].start()

        @pl.when(core == 1)
        def _():
            odd_one[part].start()

    K, V = 0, 1

    def merge(copies, slot, extra, arrived, part):
        arrived[part].wait_recv()
        add_to(slot, extra, part)
        if copies is not None:
            copies[part].start()

    def send_two(part):
        @pl.when(odd_outer == 0)
        def _():
            g_two[part].start()

    own()

    @pl.when(core == 0)
    def _():
        pass_on(K)

    @pl.when(core == 1)
    def _():
        received(ONE, K)

    slot_a, slot_b = pick(TWO, ONE), pick(ONE, TWO)
    with_keys(slot_a, 0, -slot_a, 0)

    @pl.when(core == 0)
    def _():
        received(ONE, K)

    @pl.when(core == 1)
    def _():
        g_one[V].start()
        pass_on(K)

    with_keys(slot_b, 0, -slot_b, 1)

    @pl.when(core == 0)
    def _():
        g_one[V].start()

    @pl.when(core == 1)
    def _():
        received(ONE, V)

    pass_on(V)
    with_values(slot_a, 0, -slot_a, 0)

    @pl.when(core == 0)
    def _():
        received(ONE, V)

    @pl.when(core == 1)
    def _():
        g_one[K].start()

    with_values(slot_b, 0, -slot_b, 1)

    @pl.when(core == 0)
    def _():
        g_one[K].start()

    @pl.when(core == 1)
    def _():
        received(THREE, K)
        with_keys(THREE, 0, -THREE, 0)
        g_three[V].start()
        merge(None, TWO, ONE, g_one, V)
        send_two(V)
        received(THREE, V)
        with_values(THREE, 0, -THREE, 0)
        g_three[K].start()
        merge(None, TWO, ONE, g_one, K)
        send_two(K)


    @pl.when(core == 0)
    def _():
        merge(None, TWO, THREE, g_three, V)
        send_two(V)
        merge(None, TWO, THREE, g_three, K)
        send_two(K)

        received(FOUR, K)
        with_keys(FOUR, 0, -FOUR, 0)
        g_four[V].start()
        received(THREE, K)
        with_keys(THREE, 0, -THREE, 1)
        g_three[V].start()
        received(FOUR, V)
        with_values(FOUR, 0, -FOUR, 0)
        g_four[K].start()
        received(THREE, V)
        with_values(THREE, 0, -THREE, 1)
        g_three[K].start()

    @pl.when(core == 1)
    def _():
        received(FOUR, K)
        odd_three[K].start()
        with_keys(FOUR, 0, -FOUR, 0)
        received(FOUR, V)
        odd_three[V].start()
        with_values(FOUR, 0, -FOUR, 0)
        merge(g_four, FOUR, THREE, g_three, V)
        merge(g_four, FOUR, THREE, g_three, K)

    received(OUTER, K)
    with_keys(OUTER, -1, 0, 0)
    g_outer[V].start()

    @pl.when(odd_outer == 1)
    def _():
        merge(g_two, TWO, FOUR, g_four, V)

    received(OUTER, V)
    with_values(OUTER, -1, 0, 0)
    g_outer[K].start()

    @pl.when(odd_outer == 1)
    def _():
        merge(g_two, TWO, FOUR, g_four, K)


    for h in range(HEADS):
        row = pl.ds(h * HALF, HALF)
        col = pl.ds(h * DIM, DIM)
        first, second = ordered(swapped, dq[row, pl.ds(0, DIM)], dq[row, pl.ds(DIM, DIM)])
        dq_out[pl.ds(0, HALF), col] = first * SCALE
        dq_out[pl.ds(HALF, HALF), col] = second * SCALE

    @pl.when(core == 0)
    def _():
        for part in range(2):
            g_one[part].wait_recv()
            own_acc[part] += gin[ONE, part].astype(jnp.float32)

    for part, out, factor in [(V, dv_out, 1.0), (K, dk_out, SCALE)]:
        total = own_acc[part]
        for slot, copies in [(OUTER, g_outer), (TWO, g_two)]:
            copies[part].wait_recv()
            total = total + gin[slot, part].astype(jnp.float32)
        own_acc[part] = total

        @pl.when(odd_outer == 0)
        def _():
            g_four[part].wait_recv()
            own_acc[part] += gin[FOUR, part].astype(jnp.float32)

        out[...] = own_acc[part] * factor
    for copies in (to_four, to_two, to_outer, odd_one, odd_three):
        for copy in copies:
            copy.wait_send()
    for copies in (g_two, g_four, g_outer, g_one, g_three):
        for copy in copies:
            copy.wait_send()


def write_out(*refs):
    sources, results, sem = refs[:3], refs[3:6], refs[6]
    copies = [
        pltpu.make_async_copy(src, dst, sem.at[n])
        for n, (src, dst) in enumerate(zip(sources, results))
    ]
    for copy in copies:
        copy.start()
    for copy in copies:
        copy.wait()


def local(n_outer, n_inner, queries, keys, values, outputs, out_grads, log_sum_exp, span_ids):
    block, dim = keys.shape
    width = queries.shape[1]
    heads = log_sum_exp.shape[0]
    bf16, f32 = jnp.bfloat16, jnp.float32
    in_hbm = pl.BlockSpec(memory_space=pltpu.HBM)
    in_vmem = pl.BlockSpec(memory_space=pltpu.VMEM)
    arrays = [
        pltpu.with_memory_space_constraint(a, pltpu.HBM)
        for a in (queries, keys, values, outputs, out_grads, log_sum_exp)
    ]
    shapes = [(block, width), (block, dim), (block, dim)]
    grads = pl.pallas_call(
        functools.partial(kernel, n_outer, n_inner),
        out_shape=tuple(pltpu.VMEM(shape, f32) for shape in shapes),
        in_specs=[in_hbm] * 7,
        out_specs=(in_vmem,) * 3,
        scratch_shapes=[
            pltpu.SMEM(span_ids.shape, jnp.int32),
            pltpu.VMEM((block, width), bf16),
            pltpu.VMEM((block, width), bf16),
            pltpu.VMEM((block, width), bf16),
            pltpu.VMEM((heads, block), f32),
            pltpu.VMEM((2, heads * HALF, dim), bf16),
            pltpu.VMEM((2, heads * HALF, dim), bf16),
            pltpu.VMEM((2, 8, heads * HALF), f32),
            pltpu.VMEM((6, 2, block, dim), bf16),
            pltpu.VMEM((heads * HALF, 2 * dim), f32),
            pltpu.VMEM((2, block, dim), f32),
            pltpu.VMEM((2, 2, HALF, heads * HALF), f32),
            pltpu.VMEM((6, 2, block, dim), bf16),
            pltpu.VMEM((6, 2, block, dim), bf16),
            pltpu.SemaphoreType.DMA((7,)),
            pltpu.SemaphoreType.DMA((5, 2)),
            pltpu.SemaphoreType.DMA((6, 2)),
            pltpu.SemaphoreType.DMA((6, 2)),
            pltpu.SemaphoreType.DMA((6, 2)),
        ],
        compiler_params=pltpu.CompilerParams(
            collective_id=0, has_side_effects=True, vmem_limit_bytes=48 * 1024 * 1024
        ),
        name="backward",
    )(pltpu.with_memory_space_constraint(span_ids, pltpu.HBM), *arrays)
    return pl.pallas_call(
        write_out,
        out_shape=tuple(jax.ShapeDtypeStruct(shape, f32) for shape in shapes),
        in_specs=[in_vmem] * 3,
        out_specs=(pl.BlockSpec(memory_space=pl.ANY),) * 3,
        scratch_shapes=[pltpu.SemaphoreType.DMA((3,))],
        name="write_out",
    )(*(pltpu.with_memory_space_constraint(a, pltpu.VMEM) for a in grads))


def solution(mesh):
    tokens = P(("outer", "inner"), None)
    return jax.shard_map(
        functools.partial(local, mesh.shape["outer"], mesh.shape["inner"]),
        mesh=mesh,
        in_specs=(tokens,) * 5 + (P(None, ("outer", "inner")), P()),
        out_specs=(tokens,) * 3,
        check_vma=False,
    )
```

```python
import functools
import math

import jax
import jax.numpy as jnp
from jax import lax
from jax.experimental import pallas as pl
from jax.experimental.pallas import tpu as pltpu
from jax.sharding import PartitionSpec as P

MESH = pl.DeviceIdType.MESH
HALF = 128
DIM = 128
HEADS = 8
WIDE = HEADS * HALF
NT = (((1,), (1,)), ((), ()))
NN = (((1,), (0,)), ((), ()))
TN = (((0,), (0,)), ((), ()))
LOG2E = math.log2(math.e)
SCALE = DIM ** (-0.5)

OWN, ONE, TWO, THREE, FOUR, OUTER = range(6)


def dot(a, b, dims):
    return lax.dot_general(a, b, dims, preferred_element_type=jnp.float32)


def less(a, b, shape):
    return jnp.full(shape, a, jnp.int32) < jnp.full(shape, b, jnp.int32)


def narrow(mask):
    return jnp.where(mask, 1.0, 0.0).astype(jnp.bfloat16) > 0.5


def ordered(swapped, first, second):
    return jnp.where(swapped, second, first), jnp.where(swapped, first, second)


def kernel(
    n_outer,
    n_inner,
    spans_hbm,
    q_hbm,
    k_hbm,
    v_hbm,
    o_hbm,
    g_hbm,
    lse_hbm,
    dq_out,
    dk_out,
    dv_out,
    spans,
    q_in,
    o_in,
    g_in,
    lse_in,
    qn,
    gn,
    rows,
    kv,
    dq,
    own_acc,
    weights,
    gout,
    gin,
    load_sem,
    kv_send,
    kv_recv,
    g_send,
    g_recv,
):
    outer = lax.axis_index("outer")
    inner = lax.axis_index("inner")
    core = lax.rem(inner, 2)
    odd_outer = lax.rem(outer, 2)

    def at(do, di):
        return (lax.rem(outer + do + n_outer, n_outer), lax.rem(inner + di + n_inner, n_inner))

    partner = (outer, inner + 1 - 2 * core)
    senders = [at(0, -2), at(0, -4), at(-1, 0), partner]

    barrier = pltpu.get_barrier_semaphore()
    for sender in senders:
        pl.semaphore_signal(barrier, inc=1, device_id=sender, device_id_type=MESH)

    loads = [
        pltpu.make_async_copy(src, dst, load_sem.at[n])
        for n, (src, dst) in enumerate(
            [
                (g_hbm, g_in),
                (o_hbm, o_in),
                (q_hbm, q_in),
                (lse_hbm, lse_in),
                (k_hbm, kv.at[OWN, 0]),
                (v_hbm, kv.at[OWN, 1]),
                (spans_hbm, spans),
            ]
        )
    ]
    for copy in loads:
        copy.start()

    def low_span(block):
        return jnp.minimum(spans[0, block], spans[1, block])

    def is_swapped(block, shape):
        return less(spans[1, block], spans[0, block], shape)

    def kv_copies(sources, slot, number, target):
        return [
            pltpu.make_async_remote_copy(
                src_ref=sources[part],
                dst_ref=kv.at[slot, part],
                send_sem=kv_send.at[number, part],
                recv_sem=kv_recv.at[slot, part],
                device_id=target,
                device_id_type=MESH,
            )
            for part in range(2)
        ]

    args = [k_hbm, v_hbm]
    to_four = kv_copies(args, FOUR, 0, at(0, 4))
    on_four = kv_copies([kv.at[TWO, p] for p in range(2)], FOUR, 0, at(0, 2))
    to_two = kv_copies(args, TWO, 1, at(0, 2))
    to_outer = kv_copies(args, OUTER, 2, at(1, 0))
    even_one = kv_copies(args, ONE, 3, partner)
    even_three = kv_copies([kv.at[TWO, p] for p in range(2)], THREE, 4, partner)
    odd_one = kv_copies([kv.at[TWO, p] for p in range(2)], ONE, 3, partner)
    odd_three = kv_copies([kv.at[FOUR, p] for p in range(2)], THREE, 4, partner)

    def received(slot, part):
        pltpu.make_async_remote_copy(
            src_ref=kv.at[slot, part],
            dst_ref=kv.at[slot, part],
            send_sem=kv_send.at[0, part],
            recv_sem=kv_recv.at[slot, part],
            device_id=partner,
            device_id_type=MESH,
        ).wait_recv()

    pl.semaphore_wait(barrier, len(senders))
    for part in range(2):
        to_two[part].start()

        @pl.when(core == 0)
        def _():
            even_one[part].start()

        @pl.when(odd_outer == 1)
        def _():
            to_four[part].start()

    @pl.when(odd_outer == 1)
    def _():
        for part in range(2):
            to_outer[part].start()

    for copy in loads:
        copy.wait()
    own_block = outer * n_inner + inner
    own_low = low_span(own_block)
    swapped = is_swapped(own_block, (HALF, DIM))
    swapped_low = narrow(swapped)
    ones = jnp.ones((8, DIM), jnp.bfloat16)
    for h in range(HEADS):
        col = pl.ds(h * DIM, DIM)
        row = pl.ds(h * HALF, HALF)

        def halves(ref):
            return ordered(swapped_low, ref[pl.ds(0, HALF), col], ref[pl.ds(HALF, HALF), col])

        norms = ordered(swapped[:1], lse_in[h : h + 1, :HALF], lse_in[h : h + 1, HALF:])
        for half, (q, g, o, norm) in enumerate(zip(halves(q_in), halves(g_in), halves(o_in), norms)):
            qn[half, row, :] = q
            gn[half, row, :] = g
            product = g.astype(jnp.float32) * o.astype(jnp.float32)
            top = product.astype(jnp.bfloat16)
            rest = product - top.astype(jnp.float32)
            middle = rest.astype(jnp.bfloat16)
            low = (rest - middle.astype(jnp.float32)).astype(jnp.bfloat16)
            delta = dot(ones, top, NT) + dot(ones, middle, NT) + dot(ones, low, NT)
            rows[half, 0:1, row] = delta[0:1, :]
            rows[half, 1:2, row] = norm * LOG2E

    def attend(keys, q, norm):
        return jnp.exp2(dot(keys, q, NT) * (SCALE * LOG2E) - norm)

    def score_grads(p, values, g, delta):
        return (p * (dot(values, g, NT) - delta)).astype(jnp.bfloat16)

    def halves_of(slot, part, mask):
        return ordered(mask, kv[slot, part, pl.ds(0, HALF), :], kv[slot, part, pl.ds(HALF, HALF), :])

    def own():
        key_at = lax.broadcasted_iota(jnp.int32, (HALF, WIDE), 0)
        query_at = lax.rem(lax.broadcasted_iota(jnp.int32, (HALF, WIDE), 1), HALF)
        seen = key_at <= query_at
        k_lo, k_hi = halves_of(OWN, 0, swapped_low)
        v_lo, v_hi = halves_of(OWN, 1, swapped_low)
        keys = jnp.concatenate([k_lo, k_hi], 0)
        values = jnp.concatenate([v_lo, v_hi], 0)
        p_lo = jnp.where(seen, attend(k_lo, qn[0], rows[0, 1:2, :]), 0.0)
        p_hi = attend(keys, qn[1], rows[1, 1:2, :])
        p_hi = jnp.concatenate([p_hi[:HALF], jnp.where(seen, p_hi[HALF:], 0.0)], 0)
        s_lo = score_grads(p_lo, v_lo, gn[0], rows[0, 0:1, :])
        s_hi = score_grads(p_hi, values, gn[1], rows[1, 0:1, :])
        for part, (lo, hi, other_side) in enumerate(
            [(s_lo, s_hi, qn), (p_lo.astype(jnp.bfloat16), p_hi.astype(jnp.bfloat16), gn)]
        ):
            total = dot(hi, other_side[1], NN)
            first = total[:HALF] + dot(lo, other_side[0], NN)
            own_acc[part, pl.ds(0, HALF), :], own_acc[part, pl.ds(HALF, HALF), :] = ordered(
                swapped, first, total[HALF:]
            )
        dq[:, pl.ds(0, DIM)] = dot(s_lo, k_lo, TN)
        dq[:, pl.ds(DIM, DIM)] = dot(s_hi, keys, TN)

    def sides(do, di):
        there = at(do, di)
        block = there[0] * n_inner + there[1]
        low = low_span(block)
        return (
            less(low, own_low, (HALF, DIM)),
            narrow(less(low, own_low, (WIDE, DIM))),
            less(low, own_low, (1, WIDE)),
            is_swapped(block, (HALF, DIM)),
        )

    def chosen(mask, ref, which):
        other_half = ref[1, which, :] if which is not None else ref[1]
        return jnp.where(mask, ref[0, which, :] if which is not None else ref[0], other_half)

    def put(slot, part, first, second, early, turned):
        lo = first + jnp.where(early, second, 0.0)
        hi = jnp.where(early, 0.0, second)
        for half, value in enumerate(ordered(turned, lo, hi)):
            gout[slot, part, pl.ds(half * HALF, HALF), :] = value.astype(jnp.bfloat16)

    def with_keys(slot, do, di, store):
        early, early_low, early_row, turned = sides(do, di)
        k1, k_hi = halves_of(slot, 0, narrow(turned))
        k2 = jnp.where(early_low[:HALF], k1, k_hi)
        q2 = chosen(early_low, qn, None)
        g2 = chosen(early_low, gn, None)
        norm2 = chosen(early_row, rows, pl.ds(1, 1))
        p1 = attend(k1, qn[1], rows[1, 1:2, :])
        p2 = attend(k2, q2, norm2)
        weights[store, 0] = p1
        weights[store, 1] = p2
        first = dot(p1.astype(jnp.bfloat16), gn[1], NN)
        second = dot(p2.astype(jnp.bfloat16), g2, NN)
        put(slot, 1, first, second, early, turned)

    def with_values(slot, do, di, store):
        early, early_low, early_row, turned = sides(do, di)
        k1, k_hi = halves_of(slot, 0, narrow(turned))
        v1, v_hi = halves_of(slot, 1, narrow(turned))
        k2 = jnp.where(early_low[:HALF], k1, k_hi)
        v2 = jnp.where(early_low[:HALF], v1, v_hi)
        q2 = chosen(early_low, qn, None)
        g2 = chosen(early_low, gn, None)
        delta2 = chosen(early_row, rows, pl.ds(0, 1))
        s1 = score_grads(weights[store, 0], v1, gn[1], rows[1, 0:1, :])
        s2 = score_grads(weights[store, 1], v2, g2, delta2)
        put(slot, 0, dot(s1, qn[1], NN), dot(s2, q2, NN), early, turned)
        zero = jnp.zeros_like(k1)
        wide = jnp.concatenate(
            [
                jnp.concatenate([zero, k1], 1),
                jnp.concatenate(
                    [
                        jnp.where(early_low[:HALF], k2, zero),
                        jnp.where(early_low[:HALF], zero, k2),
                    ],
                    1,
                ),
            ],
            0,
        )
        dq[...] += dot(jnp.concatenate([s1, s2], 0), wide, TN)

    def g_copies(slot, target):
        return [
            pltpu.make_async_remote_copy(
                src_ref=gout.at[slot, part],
                dst_ref=gin.at[slot, part],
                send_sem=g_send.at[slot, part],
                recv_sem=g_recv.at[slot, part],
                device_id=target,
                device_id_type=MESH,
            )
            for part in range(2)
        ]

    g_two = g_copies(TWO, at(0, -2))
    g_four = g_copies(FOUR, at(0, -4 + 2 * odd_outer))
    g_outer = g_copies(OUTER, at(-1, 0))
    g_one = g_copies(ONE, partner)
    g_three = g_copies(THREE, partner)

    def add_to(slot, extra, part):
        gout[slot, part] = (
            gout[slot, part].astype(jnp.float32) + gin[extra, part].astype(jnp.float32)
        ).astype(jnp.bfloat16)

    def pick(even, odd):
        return even + core * (odd - even)

    def pass_on(part):
        received(TWO, part)

        @pl.when(odd_outer == 0)
        def _():
            on_four[part].start()
            if part == 0:
                to_outer[0].start()
                to_outer[1].start()

        @pl.when(core == 0)
        def _():
            even_three[part].start()

        @pl.when(core == 1)
        def _():
            odd_one[part].start()

    K, V = 0, 1

    def merge(copies, slot, extra, arrived, part):
        arrived[part].wait_recv()
        add_to(slot, extra, part)
        if copies is not None:
            copies[part].start()

    def send_two(part):
        @pl.when(odd_outer == 0)
        def _():
            g_two[part].start()

    own()

    @pl.when(core == 0)
    def _():
        pass_on(K)

    @pl.when(core == 1)
    def _():
        received(ONE, K)

    slot_a, slot_b = pick(TWO, ONE), pick(ONE, TWO)
    with_keys(slot_a, 0, -slot_a, 0)

    @pl.when(core == 0)
    def _():
        received(ONE, K)

    @pl.when(core == 1)
    def _():
        g_one[V].start()
        pass_on(K)

    with_keys(slot_b, 0, -slot_b, 1)

    @pl.when(core == 0)
    def _():
        g_one[V].start()

    @pl.when(core == 1)
    def _():
        received(ONE, V)

    pass_on(V)
    with_values(slot_a, 0, -slot_a, 0)

    @pl.when(core == 0)
    def _():
        received(ONE, V)

    @pl.when(core == 1)
    def _():
        g_one[K].start()

    with_values(slot_b, 0, -slot_b, 1)

    @pl.when(core == 0)
    def _():
        g_one[K].start()

    @pl.when(core == 1)
    def _():
        received(THREE, K)
        with_keys(THREE, 0, -THREE, 0)
        g_three[V].start()
        merge(None, TWO, ONE, g_one, V)
        send_two(V)
        received(THREE, V)
        with_values(THREE, 0, -THREE, 0)
        g_three[K].start()
        merge(None, TWO, ONE, g_one, K)
        send_two(K)


    @pl.when(core == 0)
    def _():
        merge(None, TWO, THREE, g_three, V)
        send_two(V)
        merge(None, TWO, THREE, g_three, K)
        send_two(K)

        received(FOUR, K)
        with_keys(FOUR, 0, -FOUR, 0)
        g_four[V].start()
        received(THREE, K)
        with_keys(THREE, 0, -THREE, 1)
        g_three[V].start()
        received(THREE, V)
        with_values(THREE, 0, -THREE, 1)
        g_three[K].start()
        received(FOUR, V)
        with_values(FOUR, 0, -FOUR, 0)
        g_four[K].start()

    @pl.when(core == 1)
    def _():
        received(FOUR, K)
        odd_three[K].start()
        with_keys(FOUR, 0, -FOUR, 0)
        received(FOUR, V)
        odd_three[V].start()
        with_values(FOUR, 0, -FOUR, 0)
        merge(g_four, FOUR, THREE, g_three, V)
        merge(g_four, FOUR, THREE, g_three, K)

    received(OUTER, K)
    with_keys(OUTER, -1, 0, 0)
    g_outer[V].start()

    @pl.when(odd_outer == 1)
    def _():
        merge(g_two, TWO, FOUR, g_four, V)

    received(OUTER, V)
    with_values(OUTER, -1, 0, 0)
    g_outer[K].start()

    @pl.when(odd_outer == 1)
    def _():
        merge(g_two, TWO, FOUR, g_four, K)


    for h in range(HEADS):
        row = pl.ds(h * HALF, HALF)
        col = pl.ds(h * DIM, DIM)
        first, second = ordered(swapped, dq[row, pl.ds(0, DIM)], dq[row, pl.ds(DIM, DIM)])
        dq_out[pl.ds(0, HALF), col] = first * SCALE
        dq_out[pl.ds(HALF, HALF), col] = second * SCALE

    @pl.when(core == 0)
    def _():
        for part in range(2):
            g_one[part].wait_recv()
            own_acc[part] += gin[ONE, part].astype(jnp.float32)

    for part, out, factor in [(V, dv_out, 1.0), (K, dk_out, SCALE)]:
        total = own_acc[part]
        for slot, copies in [(OUTER, g_outer), (TWO, g_two)]:
            copies[part].wait_recv()
            total = total + gin[slot, part].astype(jnp.float32)
        own_acc[part] = total

        @pl.when(odd_outer == 0)
        def _():
            g_four[part].wait_recv()
            own_acc[part] += gin[FOUR, part].astype(jnp.float32)

        out[...] = own_acc[part] * factor
    for copies in (to_four, to_two, to_outer, odd_one, odd_three):
        for copy in copies:
            copy.wait_send()
    for copies in (g_two, g_four, g_outer, g_one, g_three):
        for copy in copies:
            copy.wait_send()


def write_out(*refs):
    sources, results, sem = refs[:3], refs[3:6], refs[6]
    copies = [
        pltpu.make_async_copy(src, dst, sem.at[n])
        for n, (src, dst) in enumerate(zip(sources, results))
    ]
    for copy in copies:
        copy.start()
    for copy in copies:
        copy.wait()


def local(n_outer, n_inner, queries, keys, values, outputs, out_grads, log_sum_exp, span_ids):
    block, dim = keys.shape
    width = queries.shape[1]
    heads = log_sum_exp.shape[0]
    bf16, f32 = jnp.bfloat16, jnp.float32
    in_hbm = pl.BlockSpec(memory_space=pltpu.HBM)
    in_vmem = pl.BlockSpec(memory_space=pltpu.VMEM)
    arrays = [
        pltpu.with_memory_space_constraint(a, pltpu.HBM)
        for a in (queries, keys, values, outputs, out_grads, log_sum_exp)
    ]
    shapes = [(block, width), (block, dim), (block, dim)]
    grads = pl.pallas_call(
        functools.partial(kernel, n_outer, n_inner),
        out_shape=tuple(pltpu.VMEM(shape, f32) for shape in shapes),
        in_specs=[in_hbm] * 7,
        out_specs=(in_vmem,) * 3,
        scratch_shapes=[
            pltpu.SMEM(span_ids.shape, jnp.int32),
            pltpu.VMEM((block, width), bf16),
            pltpu.VMEM((block, width), bf16),
            pltpu.VMEM((block, width), bf16),
            pltpu.VMEM((heads, block), f32),
            pltpu.VMEM((2, heads * HALF, dim), bf16),
            pltpu.VMEM((2, heads * HALF, dim), bf16),
            pltpu.VMEM((2, 8, heads * HALF), f32),
            pltpu.VMEM((6, 2, block, dim), bf16),
            pltpu.VMEM((heads * HALF, 2 * dim), f32),
            pltpu.VMEM((2, block, dim), f32),
            pltpu.VMEM((2, 2, HALF, heads * HALF), f32),
            pltpu.VMEM((6, 2, block, dim), bf16),
            pltpu.VMEM((6, 2, block, dim), bf16),
            pltpu.SemaphoreType.DMA((7,)),
            pltpu.SemaphoreType.DMA((5, 2)),
            pltpu.SemaphoreType.DMA((6, 2)),
            pltpu.SemaphoreType.DMA((6, 2)),
            pltpu.SemaphoreType.DMA((6, 2)),
        ],
        compiler_params=pltpu.CompilerParams(
            collective_id=0, has_side_effects=True, vmem_limit_bytes=48 * 1024 * 1024
        ),
        name="backward",
    )(pltpu.with_memory_space_constraint(span_ids, pltpu.HBM), *arrays)
    return pl.pallas_call(
        write_out,
        out_shape=tuple(jax.ShapeDtypeStruct(shape, f32) for shape in shapes),
        in_specs=[in_vmem] * 3,
        out_specs=(pl.BlockSpec(memory_space=pl.ANY),) * 3,
        scratch_shapes=[pltpu.SemaphoreType.DMA((3,))],
        name="write_out",
    )(*(pltpu.with_memory_space_constraint(a, pltpu.VMEM) for a in grads))


def solution(mesh):
    tokens = P(("outer", "inner"), None)
    return jax.shard_map(
        functools.partial(local, mesh.shape["outer"], mesh.shape["inner"]),
        mesh=mesh,
        in_specs=(tokens,) * 5 + (P(None, ("outer", "inner")), P()),
        out_specs=(tokens,) * 3,
        check_vma=False,
    )
```
